256 devices in a mesh: dp: 2 (over core), expert: 16 (over x, y), tensor: 8 (over z).
Axes of the slice: x: 4, y: 4, z: 8, core: 2. Of those that a mesh axis runs over, the one named last changes fastest.
Arguments:
- layer_input: bfloat16 [4096, 3584], P(('dp', 'expert'), 'tensor'), may hold values from -6 to 6
- cotangent: bfloat16 [4096, 3584], P(('dp', 'expert'), 'tensor'), may hold values from -1.25 to 1.25
- route_probs: float32 [4096, 2], P(('dp', 'expert')), may hold values from 0.1 to 1
- routes: int32 [4096, 2], P(('dp', 'expert')), may hold values from 0 to 15, all different within a row; in each aligned block of 128 rows (0 to 127, 128 to 255, ...) at most 20 rows name the same one
- shared_gate: bfloat16 [3584, 2432], P('dp', 'tensor'), may hold values from -0.09375 to 0.09375
- shared_up: bfloat16 [3584, 2432], P('dp', 'tensor'), may hold values from -0.09375 to 0.09375
- shared_down: bfloat16 [2432, 3584], P('tensor', 'dp'), may hold values from -0.125 to 0.125
- routed_gate: bfloat16 [16, 3584, 2432], P('expert', 'dp', 'tensor'), may hold values from -0.09375 to 0.09375
- routed_up: bfloat16 [16, 3584, 2432], P('expert', 'dp', 'tensor'), may hold values from -0.09375 to 0.09375
- routed_down: bfloat16 [16, 2432, 3584], P('expert', 'tensor', 'dp'), may hold values from -0.125 to 0.125
Outputs:
- input_grad: bfloat16 [4096, 3584], P(('dp', 'expert'), 'tensor')
- prob_grad: float32 [4096, 2], P(('dp', 'expert'))
- grad_gate: bfloat16 [3584, 2432], P(('dp', 'expert'), 'tensor')
- grad_up: bfloat16 [3584, 2432], P(('dp', 'expert'), 'tensor')
- grad_down: bfloat16 [2432, 3584], P('tensor', ('dp', 'expert'))
- delta_gate: bfloat16 [16, 3584, 2432], P('expert', 'dp', 'tensor')
- delta_up: bfloat16 [16, 3584, 2432], P('expert', 'dp', 'tensor')
- delta_down: bfloat16 [16, 2432, 3584], P('expert', 'tensor', 'dp')
The draws below stay inside these ranges and needn't reach their ends.
Inputs may be any that keep to these rules, and one draw needn't show every extreme that they name: `routes`: each token names 2 different experts. Among the 128 rows of one block, no expert is named more than 20 times, and in every draw some expert is named exactly 20 times in some block.
All inputs are finite; a program needn't handle non-finite values.
Results may differ from the reference program's by a relative error of at most 0.022.
Values may be sent and summed in bfloat16 or wider, within the bound.
No kernel may reach another device: no remote copies, remote signals or barrier semaphores. Data moves between devices by JAX's collectives and lax.ppermute only.
A program may use at most 192 MiB of HBM per device.

```python
import math
import jax
import jax.numpy as jnp
import numpy as np
from jax import lax

D = 3584
HID = 2432
TOP = 2
TOK_DEV = 128
EXPERTS = 16
CAP = 20
TOKENS = 4096
N_DP = 2
N_EXPERT = 16


def spiked(values, rng, source, target, shards_of, factor):
    def block_of(axis_at):
        return (jnp.arange(values.shape[axis_at]) // (values.shape[axis_at] // shards_of)).reshape((-1,) + (1,) * (values.ndim - 1 - axis_at))

    first = jax.random.permutation(rng, shards_of)[block_of(target)]
    other_side = (block_of(target) + shards_of // 2) % shards_of
    return jnp.where((block_of(source) == first) | (block_of(source) == other_side), factor * values, values)


def levels(key, extent, split, least, top_value):
    factor_of, own = 1.0, jax.random.fold_in(key, 6)
    for dim, shards_of in split:
        draws = jnp.exp(jax.random.uniform(jax.random.fold_in(own, dim), (shards_of,), jnp.float32, least / len(split), top_value / len(split)))
        factor_of = factor_of * jnp.repeat(draws, extent[dim] // shards_of).reshape([-1 if axis == dim else 1 for axis in range(len(extent))])
    return factor_of


def assign_block(key, own, number, rows, count, top, reach, skew):
    ranking = jax.random.permutation(key, count)
    heavy_load, common = load_shares(count, rows * top, reach, skew, True), load_shares(count, rows * top, reach, skew, False)
    places = jnp.arange(count)

    def named(lengths, rotation):
        used = int((lengths > 0).sum())
        fixed = max(1, used // 4)
        passed = fixed + (places - fixed + rotation * (used - fixed)) % max(1, count - fixed)
        return jnp.zeros((count,), jnp.int32).at[ranking[jnp.where(places < fixed, places, passed)]].set(jnp.asarray(lengths, jnp.int32))

    lengths = jnp.where(number % 4 == 0, named(heavy_load, number // 4), named(common, number - number // 4 - 1))
    mixed = jax.random.permutation(jax.random.fold_in(own, 3), count)
    source_of, receiver = mixed[0:count // 2 * 2:2], mixed[1:count // 2 * 2:2]
    room = jnp.minimum(lengths[source_of] - 1, reach - lengths[receiver]) // 2
    room = jnp.where((source_of == ranking[0]) | (receiver == ranking[0]) | (lengths[receiver] == 0), 0, jnp.maximum(room, 0))
    passed = jax.random.randint(jax.random.fold_in(own, 4), (count // 2,), 0, 1 << 20) % (room + 1)
    lengths = lengths.at[source_of].add(-passed).at[receiver].add(passed)
    members = jnp.searchsorted(jnp.cumsum(lengths), jnp.arange(rows * top), side="right").astype(jnp.int32)
    table = members.reshape(top, rows).T
    table = table[jax.random.permutation(jax.random.fold_in(own, 1), rows)]
    rotation = jax.random.randint(jax.random.fold_in(own, 2), (rows, 1), 0, top)
    return jnp.take_along_axis(table, (jnp.arange(top)[None, :] + rotation) % top, axis=1)


def load_shares(number_of, total, limit, lean, full):
    weights = [(1 << 20) // math.isqrt(grade ** lean) + 1 for grade in range(1, number_of + 1)]
    largest = limit if full else min(limit, max(-(-total // number_of), total * weights[0] // sum(weights)))
    least = 1 if total - largest >= number_of - 1 else 0
    given, surplus = [largest] + [least] * (number_of - 1), total - largest - least * (number_of - 1)
    while surplus > 0:
        free = [i for i in range(1, number_of) if given[i] < largest] or [i for i in range(1, number_of) if given[i] < limit]
        mass, budget = sum([weights[i] for i in free]), surplus
        for i in free:
            addition = min(limit - given[i], max(1, budget * weights[i] // mass), surplus)
            given[i] = given[i] + addition
            surplus = surplus - addition
    return np.array(given)


def centred(stream_key, dims, deviation, most, split=(), held_as=jnp.bfloat16):
    loudness = levels(stream_key, dims, split, -0.22, 0.18) if split else 1.0
    values = jax.random.normal(stream_key, dims, jnp.float32) * deviation * loudness
    return jnp.minimum(jnp.maximum(values, -most), most).astype(held_as)


def bell_draw_with(own_key, shape, deviation, reach, cuts, heavy, held_as=jnp.bfloat16):
    drawn = deviation * jax.random.normal(own_key, shape, jnp.float32)
    if cuts:
        drawn = drawn * levels(own_key, shape, cuts, -0.22, 0.18)
    return jnp.clip(spiked(drawn, jax.random.fold_in(own_key, 3), *heavy), -reach, reach).astype(held_as)


def setup_inputs(seed: int = 0) -> dict:
    streams_of = jax.random.split(jax.random.key(seed), 11)
    layer_input = centred(streams_of[0], (TOKENS, D), 1.0, 6.0, ((0, 32), (1, 8)))
    cotangent = bell_draw_with(streams_of[1], (TOKENS, D), 0.1, 1.25, ((0, 32), (1, 8)), (0, 1, 32, 2.75))
    route_probs = jnp.clip(0.1 + 0.9 * jax.random.uniform(streams_of[2], (TOKENS, TOP), jnp.float32) ** levels(streams_of[2], (TOKENS, TOP), ((0, 32),), -0.2, 0.2), 0.1, 1.0)
    routes_keys = jax.random.split(jax.random.fold_in(streams_of[3], 1), TOKENS // TOK_DEV)
    routes_turns = jax.random.permutation(jax.random.fold_in(streams_of[3], 3), TOKENS // TOK_DEV)
    routes = jax.vmap(lambda own, number: assign_block(jax.random.fold_in(streams_of[3], 2), own, number, TOK_DEV, EXPERTS, TOP, CAP, 2))(routes_keys, routes_turns).reshape((TOKENS, TOP))
    shared_gate = centred(streams_of[4], (D, HID), D ** -0.5, 0.09375, ((0, 2), (1, 8)))
    shared_up = centred(streams_of[5], (D, HID), D ** -0.5, 0.09375, ((0, 2), (1, 8)))
    shared_down = centred(streams_of[6], (HID, D), HID ** -0.5, 0.125, ((0, 8), (1, 2)))
    routed_gate = centred(streams_of[7], (EXPERTS, D, HID), D ** -0.5, 0.09375, ((0, 16), (1, 2), (2, 8)))
    routed_up = centred(streams_of[8], (EXPERTS, D, HID), D ** -0.5, 0.09375, ((0, 16), (1, 2), (2, 8)))
    routed_down = centred(streams_of[9], (EXPERTS, HID, D), HID ** -0.5, 0.125, ((0, 16), (1, 8), (2, 2)))
    return dict(layer_input=layer_input, cotangent=cotangent, route_probs=route_probs, routes=routes, shared_gate=shared_gate, shared_up=shared_up, shared_down=shared_down, routed_gate=routed_gate, routed_up=routed_up, routed_down=routed_down)


def silu_parts(pre_gate):
    sigmoid = jax.nn.sigmoid(pre_gate)
    return pre_gate * sigmoid, sigmoid * (1.0 + pre_gate * (1.0 - sigmoid))


def local_backward(rows_in, rows_out, scale_rows, w_gate, w_up, w_down):
    pre_gate = jnp.einsum("td,dh->th", rows_in, w_gate, preferred_element_type=jnp.float32)
    pre_up = jnp.einsum("td,dh->th", rows_in, w_up, preferred_element_type=jnp.float32)
    act_gate, act_slope = silu_parts(pre_gate)
    hidden = (act_gate * pre_up).astype(jnp.bfloat16)
    from_down = jnp.einsum("td,hd->th", rows_out, w_down, preferred_element_type=jnp.float32)
    probe_local = jnp.sum(hidden.astype(jnp.float32) * from_down, axis=1)
    hidden_back = scale_rows[:, None] * from_down
    gate_back = (hidden_back * pre_up * act_slope).astype(jnp.bfloat16)
    up_back = (hidden_back * act_gate).astype(jnp.bfloat16)
    scaled_out = (scale_rows[:, None] * rows_out.astype(jnp.float32)).astype(jnp.bfloat16)
    rows_back = jnp.einsum("th,dh->td", gate_back, w_gate, preferred_element_type=jnp.float32)
    rows_back = rows_back + jnp.einsum("th,dh->td", up_back, w_up, preferred_element_type=jnp.float32)
    term_gate = jnp.einsum("td,th->dh", rows_in, gate_back, preferred_element_type=jnp.float32).astype(jnp.bfloat16)
    term_up = jnp.einsum("td,th->dh", rows_in, up_back, preferred_element_type=jnp.float32).astype(jnp.bfloat16)
    term_down = jnp.einsum("th,td->hd", hidden, scaled_out, preferred_element_type=jnp.float32).astype(jnp.bfloat16)
    return probe_local, rows_back, (term_gate, term_up, term_down)


def widen(terms):
    kept = lax.optimization_barrier(terms)
    return tuple(item.astype(jnp.float32) for item in kept)


def pick_rows(table, index):
    return table[index]


def per_expert(values):
    tail = values.shape[2:]
    grid = values.reshape((N_DP, N_EXPERT, EXPERTS, CAP) + tail)
    grid = jnp.moveaxis(grid, 2, 0)
    return grid.reshape((EXPERTS, N_DP, N_EXPERT * CAP) + tail)


def per_block(values):
    tail = values.shape[3:]
    grid = values.reshape((EXPERTS, N_DP, N_EXPERT, CAP) + tail)
    grid = jnp.moveaxis(grid, 0, 2)
    return grid.reshape((N_DP * N_EXPERT, EXPERTS * CAP) + tail)


def reference(layer_input, cotangent, route_probs, routes, shared_gate, shared_up, shared_down, routed_gate, routed_up, routed_down):
    blocks = N_DP * N_EXPERT
    block_in = layer_input.reshape(blocks, TOK_DEV, D)
    block_out = cotangent.reshape(blocks, TOK_DEV, D)
    unit_scale = jnp.ones((TOK_DEV,), jnp.float32)

    def dense_step(carry, item):
        rows_in, rows_out = item
        probe_local, rows_back, terms = local_backward(rows_in, rows_out, unit_scale, shared_gate, shared_up, shared_down)
        wide_terms = widen(terms)
        return tuple(left + right for left, right in zip(carry, wide_terms)), rows_back

    start = (jnp.zeros((D, HID), jnp.float32), jnp.zeros((D, HID), jnp.float32), jnp.zeros((HID, D), jnp.float32))
    dense_sums, dense_rows = lax.scan(dense_step, start, (block_in, block_out))

    flat_routes = routes.reshape(blocks, TOK_DEV * TOP)
    expert_ids = jnp.arange(EXPERTS, dtype=jnp.int32)
    onehot = (flat_routes[:, :, None] == expert_ids[None, None, :]).astype(jnp.int32)
    earlier = jnp.cumsum(onehot, axis=1) - onehot
    slot_id = (flat_routes * CAP + jnp.sum(earlier * onehot, axis=2)).astype(jnp.int32)
    slot_ids = jnp.arange(EXPERTS * CAP, dtype=jnp.int32)
    matches = slot_id[:, None, :] == slot_ids[None, :, None]
    match_int = matches.astype(jnp.int32)
    source = jnp.sum(match_int * jnp.arange(TOK_DEV * TOP, dtype=jnp.int32)[None, None, :], axis=2)
    filled = jnp.sum(match_int, axis=2) > 0
    token_index = (source // TOP).astype(jnp.int32)
    slot_prob = jnp.sum(jnp.where(matches, route_probs.reshape(blocks, 1, TOK_DEV * TOP), jnp.zeros((), jnp.float32)), axis=2)
    slot_prob = lax.optimization_barrier(slot_prob.astype(jnp.bfloat16)).astype(jnp.float32)
    zero_value = jnp.zeros((), jnp.bfloat16)
    picked_in = jnp.where(filled[:, :, None], jax.vmap(pick_rows)(block_in, token_index), zero_value)
    picked_out = jnp.where(filled[:, :, None], jax.vmap(pick_rows)(block_out, token_index), zero_value)

    def one_expert(item):
        rows_in, rows_out, rows_prob, w_gate, w_up, w_down = item
        sums = (jnp.zeros((D, HID), jnp.float32), jnp.zeros((D, HID), jnp.float32), jnp.zeros((HID, D), jnp.float32))
        probes = []
        backs = []
        for data_group in range(N_DP):
            probe_local, rows_back, terms = local_backward(rows_in[data_group], rows_out[data_group], rows_prob[data_group], w_gate, w_up, w_down)
            wide_terms = widen(terms)
            sums = tuple(left + right for left, right in zip(sums, wide_terms))
            probes.append(probe_local)
            backs.append(rows_back)
        return (jnp.stack(probes), jnp.stack(backs), sums[0].astype(jnp.bfloat16), sums[1].astype(jnp.bfloat16), sums[2].astype(jnp.bfloat16))

    probe_all, rows_all, delta_gate, delta_up, delta_down = lax.map(one_expert, (per_expert(picked_in), per_expert(picked_out), per_expert(slot_prob), routed_gate, routed_up, routed_down))
    slot_rows = per_block(rows_all)
    slot_probe = per_block(probe_all)
    routed_sum = jax.vmap(pick_rows)(slot_rows, slot_id).reshape(blocks, TOK_DEV, TOP, D).sum(axis=2)
    input_grad = (dense_rows + routed_sum).reshape(TOKENS, D).astype(jnp.bfloat16)
    prob_grad = jax.vmap(pick_rows)(slot_probe, slot_id).reshape(TOKENS, TOP)
    return (input_grad, prob_grad, dense_sums[0].astype(jnp.bfloat16), dense_sums[1].astype(jnp.bfloat16), dense_sums[2].astype(jnp.bfloat16), delta_gate, delta_up, delta_down)
```

```python
import jax
import jax.numpy as jnp
from jax import lax
from jax.sharding import PartitionSpec as P

TOP = 2
STRIDE_PAD = 4
F32 = jnp.float32
BF16 = jnp.bfloat16


def product(spec, left, right):
    return jnp.einsum(spec, left, right, preferred_element_type=F32)


def silu_parts(pre_gate):
    sigmoid = jax.nn.sigmoid(pre_gate)
    return (pre_gate * sigmoid, sigmoid * (1.0 + pre_gate * (1.0 - sigmoid)))


def swap(values):
    return lax.ppermute(values, "dp", [(0, 1), (1, 0)])


def ring(values, shift):
    size = lax.axis_size("tensor")
    return lax.ppermute(values, "tensor", [(i, (i + shift) % size) for i in range(size)])


def gather_ring(chunk):
    size = lax.axis_size("tensor")
    here = lax.axis_index("tensor")
    full = jnp.zeros((size,) + chunk.shape, chunk.dtype)

    def put(full, piece, source):
        return lax.dynamic_update_slice(full, piece[None], (source,) + (0,) * chunk.ndim)

    full = put(full, chunk, here)
    right = left = chunk
    for step in range(1, size // 2 + 1):
        right = ring(right, 1)
        full = put(full, right, lax.rem(here - step + size, size))
        if step < size - size // 2:
            left = ring(left, -1)
            full = put(full, left, lax.rem(here + step, size))
    return full


def pair(own, other, axis):
    first = lax.axis_index("dp") == 0
    return jnp.concatenate(
        [jnp.where(first, own, other), jnp.where(first, other, own)], axis=axis
    )


def halves(values, axis):
    half = values.shape[axis] // 2
    index = lax.axis_index("dp")
    return (
        lax.dynamic_slice_in_dim(values, index * half, half, axis),
        lax.dynamic_slice_in_dim(values, (1 - index) * half, half, axis),
    )


def activations(pre_gate, pre_up, from_down, scale):
    act_gate, act_slope = silu_parts(pre_gate)
    hidden = (act_gate * pre_up).astype(BF16)
    hidden_back = from_down if scale is None else scale[:, None] * from_down
    gate_back = (hidden_back * pre_up * act_slope).astype(BF16)
    up_back = (hidden_back * act_gate).astype(BF16)
    return hidden, gate_back, up_back


def local(
    layer_input,
    cotangent,
    route_probs,
    routes,
    shared_gate,
    shared_up,
    shared_down,
    routed_gate,
    routed_up,
    routed_down,
):
    tok_rows, feats = layer_input.shape
    experts = lax.axis_size("expert")
    capacity = 5 * TOP * tok_rows // (4 * experts)
    stride = capacity + STRIDE_PAD
    slots = experts * stride

    both = jnp.concatenate([layer_input.T, cotangent.T], axis=0)
    dense = gather_ring(both)
    width = dense.shape[0] * feats
    full_in = dense[:, :feats].reshape(width, tok_rows)
    full_out = dense[:, feats:].reshape(width, tok_rows)

    expert_ids = jnp.arange(experts, dtype=jnp.int32)
    named = (routes[:, :, None] == expert_ids).astype(F32)
    lower = jnp.tri(tok_rows, k=-1, dtype=F32)
    earlier = product("nm,me->ne", lower, named.sum(axis=1))
    rank = (earlier[:, None, :] * named).sum(axis=2).astype(jnp.int32)
    slot_id = routes * stride + rank
    picks = slot_id[:, :, None] == jnp.arange(slots, dtype=jnp.int32)
    match = picks.astype(BF16).sum(axis=1)
    slot_prob = jnp.where(picks, route_probs[:, :, None], 0.0).sum(axis=(0, 1)).astype(BF16)

    row_of = jnp.arange(stride, dtype=jnp.int32)[None, :, None]
    sliced = product("ns,fn->sf", match, both).astype(BF16).reshape(experts, stride, 2 * feats)
    scale_row = jnp.pad(
        slot_prob.reshape(experts, stride), ((0, 0), (0, 2 * feats - stride))
    )
    sliced = jnp.where(row_of == capacity, scale_row[:, None, :], sliced)
    arrived = lax.all_to_all(sliced, "expert", split_axis=0, concat_axis=0, tiled=True)
    slot_scale = arrived[:, capacity, :stride].reshape(slots).astype(F32)
    compact = arrived[:, :capacity, :].reshape(experts * capacity, 2 * feats)
    slices = lax.all_gather(compact, "tensor", axis=0, tiled=False)

    def whole_rows(part):
        rows = part.reshape(part.shape[0], experts, capacity, feats)
        rows = rows.transpose(1, 2, 0, 3).reshape(experts, capacity, width)
        return jnp.pad(rows, ((0, 0), (0, STRIDE_PAD), (0, 0))).reshape(slots, width)

    slot_in = whole_rows(slices[:, :, :feats])
    slot_out = whole_rows(slices[:, :, feats:])

    gate_full = pair(shared_gate, swap(shared_gate), 0)
    up_full = pair(shared_up, swap(shared_up), 0)
    down_full = pair(shared_down, swap(shared_down), 1)
    exp_gate = pair(routed_gate[0], swap(routed_gate[0]), 0)
    exp_up = pair(routed_up[0], swap(routed_up[0]), 0)
    exp_down = pair(routed_down[0], swap(routed_down[0]), 1)

    pre_gate = product("dn,dh->nh", full_in, gate_full)
    pre_up = product("dn,dh->nh", full_in, up_full)
    from_down = product("dn,hd->nh", full_out, down_full)
    hidden, gate_back, up_back = activations(pre_gate, pre_up, from_down, None)
    in_own, in_other = halves(full_in, 0)
    out_own, out_other = halves(full_out, 0)
    backs = jnp.concatenate([gate_back, up_back], axis=1)
    sums_other = swap(product("dn,nh->dh", in_other, backs).astype(BF16))
    down_other = swap(product("dn,nh->dh", out_other, hidden).astype(BF16))
    sums = (product("dn,nh->dh", in_own, backs) + sums_other.astype(F32)).astype(BF16)
    down = (product("dn,nh->dh", out_own, hidden) + down_other.astype(F32)).astype(BF16)
    terms = jnp.concatenate([sums, down], axis=1)
    terms = terms.reshape(experts, terms.shape[0] // experts, terms.shape[1])
    terms = lax.all_to_all(terms, "expert", split_axis=0, concat_axis=0, tiled=True)
    terms = terms.astype(F32).sum(axis=0).astype(BF16)
    units = hidden.shape[1]
    grad_gate = terms[:, :units]
    grad_up = terms[:, units : 2 * units]
    grad_down = terms[:, 2 * units :].T
    dense_rows = product("dh,nh->dn", gate_full, gate_back) + product(
        "dh,nh->dn", up_full, up_back
    )

    pre_gate = product("sd,dh->sh", slot_in, exp_gate)
    pre_up = product("sd,dh->sh", slot_in, exp_up)
    from_down = product("sd,hd->sh", slot_out, exp_down)
    hidden, gate_back, up_back = activations(pre_gate, pre_up, from_down, slot_scale)
    probe = (hidden.astype(F32) * from_down).sum(axis=1)
    rows_back = product("sh,dh->sd", gate_back, exp_gate) + product("sh,dh->sd", up_back, exp_up)
    high = probe.astype(BF16)
    low = (probe - high.astype(F32)).astype(BF16)
    probe_row = jnp.concatenate([high.reshape(experts, stride), low.reshape(experts, stride)], 1)
    probe_row = jnp.pad(probe_row, ((0, 0), (0, width - 2 * stride)))
    sent = jnp.where(
        row_of == capacity,
        probe_row[:, None, :],
        rows_back.astype(BF16).reshape(experts, stride, width),
    )
    back = lax.all_to_all(sent, "expert", split_axis=0, concat_axis=0, tiled=True)

    scaled_out = (slot_scale[:, None] * slot_out.astype(F32)).astype(BF16)
    in_own, in_other = halves(slot_in, 1)
    out_own, out_other = halves(scaled_out, 1)

    def reduced(spec, own, other, backs):
        arrived = swap(product(spec, other, backs).astype(BF16))
        return (product(spec, own, backs) + arrived.astype(F32)).astype(BF16)[None]

    delta_gate = reduced("sd,sh->dh", in_own, in_other, gate_back)
    delta_up = reduced("sd,sh->dh", in_own, in_other, up_back)
    delta_down = reduced("sd,sh->hd", out_own, out_other, hidden)

    home_probe = back[:, capacity, : 2 * stride].astype(F32)
    home_probe = (home_probe[:, :stride] + home_probe[:, stride:]).reshape(slots)
    prob_part = jnp.where(picks, home_probe, 0.0).sum(axis=2).T
    high = prob_part.astype(BF16)
    low = (prob_part - high.astype(F32)).astype(BF16)
    extra = jnp.pad(jnp.concatenate([high, low], axis=0), ((0, 16 - 2 * TOP), (0, 0)))
    routed_sum = product("sd,ns->dn", back.reshape(slots, width), match)
    total = (dense_rows + routed_sum).astype(BF16).reshape(-1, feats, tok_rows)
    total = jnp.concatenate(
        [total, jnp.broadcast_to(extra, (total.shape[0],) + extra.shape)], axis=1
    )
    total = lax.all_to_all(total, "tensor", split_axis=0, concat_axis=0, tiled=True)
    total = total.astype(F32).sum(axis=0)
    input_grad = total[:feats].T.astype(BF16)
    prob_grad = (total[feats : feats + TOP] + total[feats + TOP : feats + 2 * TOP]).T
    return (
        input_grad,
        prob_grad,
        grad_gate,
        grad_up,
        grad_down,
        delta_gate,
        delta_up,
        delta_down,
    )


def solution(mesh):
    return jax.shard_map(
        local,
        mesh=mesh,
        in_specs=(
            P(("dp", "expert"), "tensor"),
            P(("dp", "expert"), "tensor"),
            P(("dp", "expert"), None),
            P(("dp", "expert"), None),
            P("dp", "tensor"),
            P("dp", "tensor"),
            P("tensor", "dp"),
            P("expert", "dp", "tensor"),
            P("expert", "dp", "tensor"),
            P("expert", "tensor", "dp"),
        ),
        out_specs=(
            P(("dp", "expert"), "tensor"),
            P(("dp", "expert"), None),
            P(("dp", "expert"), "tensor"),
            P(("dp", "expert"), "tensor"),
            P("tensor", ("dp", "expert")),
            P("expert", "dp", "tensor"),
            P("expert", "dp", "tensor"),
            P("expert", "tensor", "dp"),
        ),
        check_vma=False,
    )
```

```python
import functools

import jax
import jax.numpy as jnp
from jax import lax
from jax.experimental import pallas as pl
from jax.experimental.pallas import tpu as pltpu
from jax.sharding import PartitionSpec as P

TOP = 2
TILE = 16
LANES = 128
VMEM_LIMIT = 56 * 1024 * 1024
F32 = jnp.float32
BF16 = jnp.bfloat16


def product(spec, left, right):
    return jnp.einsum(spec, left, right, preferred_element_type=F32)


def swap(values):
    return lax.ppermute(values, "dp", [(0, 1), (1, 0)])


def ring(values, shift):
    size = lax.axis_size("tensor")
    return lax.ppermute(values, "tensor", [(i, (i + shift) % size) for i in range(size)])


def single_ring(chunk, steps, state=None):
    size = lax.axis_size("tensor")
    right, left = state or (chunk, chunk)
    pieces = []
    for step in steps:
        right = ring(right, 1)
        pieces.append((right, size - step))
        if step < size - step:
            left = ring(left, -1)
            pieces.append((left, step))
    return pieces, (right, left)


def halves(values, axis):
    half = values.shape[axis] // 2
    index = lax.axis_index("dp")
    return (
        lax.dynamic_slice_in_dim(values, index * half, half, axis),
        lax.dynamic_slice_in_dim(values, (1 - index) * half, half, axis),
    )


def sigmoid_parts(pre_gate):
    sigmoid = 1.0 / (1.0 + jnp.exp(jnp.minimum(-pre_gate, 80.0)))
    return pre_gate * sigmoid, sigmoid * (1.0 + pre_gate * (1.0 - sigmoid))


def select(mask):
    return jnp.where(mask, 1.0, 0.0).astype(BF16)


def contract(left, right, left_dim, right_dim):
    return lax.dot_general(
        left, right, (((left_dim,), (right_dim,)), ((), ())), preferred_element_type=F32
    )


def costs(micros):
    return pl.CostEstimate(flops=1, bytes_accessed=int(micros * 3.5e6), transcendentals=0)


def shape_of(shape, dtype=BF16):
    return jax.ShapeDtypeStruct(shape, dtype)


def params():
    return pltpu.CompilerParams(
        dimension_semantics=("arbitrary",), vmem_limit_bytes=VMEM_LIMIT
    )


def dispatch_kernel(capacity, routes_ref, probs_ref, both_ref, folded_ref, places_ref):
    tokens = routes_ref.shape[1]
    main, wide = folded_ref.shape
    feats = both_ref.shape[0]
    left = capacity - TILE
    quarters = TILE // left
    piece = feats // quarters
    lane = lax.broadcasted_iota(jnp.int32, (tokens, LANES), 1)
    row = lax.broadcasted_iota(jnp.int32, (tokens, tokens), 0)
    column = lax.broadcasted_iota(jnp.int32, (tokens, tokens), 1)

    def column_of(ref, k):
        return jnp.broadcast_to(ref[k : k + 1, :].astype(F32), (tokens, tokens)).T

    routed = [column_of(routes_ref, k).astype(jnp.int32) for k in range(TOP)]
    probs = [column_of(probs_ref, k).astype(BF16).astype(F32)[:, :LANES] for k in range(TOP)]
    named = [lane == routed[k][:, :LANES] for k in range(TOP)]
    earlier = jnp.dot(
        select(row > column), select(named[0] | named[1]), preferred_element_type=F32
    )
    slot = lax.broadcasted_iota(jnp.int32, (tokens, main), 1)
    near, far = [], []
    for k in range(TOP):
        rank = jnp.sum(jnp.where(named[k], earlier, 0.0), axis=1, keepdims=True).astype(jnp.int32)
        first = routed[k][:, :1] * TILE + rank
        near.append(jnp.where(rank < TILE, first, -main))
        far.append(jnp.where(rank < TILE, -main, first - TILE))
    for k in range(TOP):
        places_ref[:, k : k + 1] = near[k]
        places_ref[:, TOP + k : TOP + k + 1] = far[k]
    near = [select(slot == place) for place in near]
    folded_ref[:, :feats] = contract(near[0] + near[1], both_ref[...], 0, 1).astype(BF16)
    rest = jnp.zeros((main, piece), F32)
    for quarter in range(quarters):
        picked = [select(slot == place + quarter * left) for place in far]
        rest += contract(
            picked[0] + picked[1], both_ref[quarter * piece : (quarter + 1) * piece, :], 0, 1
        )
    folded_ref[:, feats : feats + piece] = rest.astype(BF16)
    scales = jnp.zeros((main, LANES), F32)
    for k in range(TOP):
        scales += contract(near[k], jnp.where(lane == 0, probs[k], 0.0).astype(BF16), 0, 0)
        scales += contract(
            select(slot == far[k]), jnp.where(lane == 1, probs[k], 0.0).astype(BF16), 0, 0
        )
    folded_ref[:, feats + piece :] = scales[:, : wide - feats - piece].astype(BF16)


def dispatch(routes, probs, both, experts, capacity):
    feats, tokens = both.shape
    wide = feats + feats * (capacity - TILE) // TILE
    wide = (wide // LANES + 1) * LANES
    return pl.pallas_call(
        functools.partial(dispatch_kernel, capacity),
        out_shape=[
            shape_of((experts * TILE, wide)),
            shape_of((tokens, 2 * TOP), jnp.int32),
        ],
        compiler_params=pltpu.CompilerParams(vmem_limit_bytes=VMEM_LIMIT),
        cost_estimate=costs(3),
    )(routes, probs, both)


def dense_kernel(distances, coords_ref, *refs):
    pieces = refs[: len(distances)]
    (
        gate_own_ref,
        gate_other_ref,
        up_own_ref,
        up_other_ref,
        down_own_ref,
        down_other_ref,
        own_ref,
        backs_ref,
        hidden_ref,
        pair_terms_ref,
        down_terms_ref,
        rows,
        arrivals,
        pre,
        from_down,
    ) = refs[len(distances) :]
    step = pl.program_id(0)
    size, wide, tokens = rows.shape
    parts = size // 4
    feats = wide // 2
    units = hidden_ref.shape[0]
    block = parts * feats
    place = lax.rem(coords_ref[1] * 2 + jnp.where(step < 4, step, step - 2), 4)

    @pl.when(step == 0)
    def _():
        for ref, distance in zip(pieces, distances):
            origin = lax.rem(coords_ref[0] + distance, size)
            pltpu.make_async_copy(ref, rows.at[origin], arrivals.at[origin]).start()
        pre[...] = jnp.zeros_like(pre)
        from_down[...] = jnp.zeros_like(from_down)

    @pl.when(step < 4)
    def _():
        for part in range(parts):
            origin = place * parts + part
            pltpu.make_async_copy(pieces[0], rows.at[origin], arrivals.at[origin]).wait()

    @pl.when(step < 2)
    def _():
        own_ref[...] = rows[pl.ds(place * parts, parts)]

    rows_in = rows[pl.ds(place * parts, parts), :feats, :].reshape(block, tokens)
    rows_out = rows[pl.ds(place * parts, parts), feats:, :].reshape(block, tokens)

    def forward(gate_ref, up_ref, down_ref):
        pair = jnp.concatenate([gate_ref[...], up_ref[...]], axis=0)
        pre[...] += jnp.dot(pair, rows_in, preferred_element_type=F32)
        from_down[...] += jnp.dot(down_ref[...], rows_out, preferred_element_type=F32)

    @pl.when(step < 2)
    def _():
        forward(gate_own_ref, up_own_ref, down_own_ref)

    @pl.when((step >= 2) & (step < 4))
    def _():
        forward(gate_other_ref, up_other_ref, down_other_ref)

    @pl.when(step == 3)
    def _():
        act, slope = sigmoid_parts(pre[:units])
        raised = pre[units:]
        back = from_down[...]
        hidden_ref[...] = (act * raised).astype(BF16)
        backs_ref[:units] = (back * raised * slope).astype(BF16)
        backs_ref[units:] = (back * act).astype(BF16)

    @pl.when(step >= 4)
    def _():
        backs = contract(rows_in, backs_ref[...], 1, 1).astype(BF16)
        down = contract(rows_out, hidden_ref[...], 1, 1).astype(BF16)
        empty = pair_terms_ref.shape[1] - 2 * units
        pair_terms_ref[...] = jnp.concatenate([backs, jnp.zeros((block, empty), BF16)], axis=1)
        empty = down_terms_ref.shape[1] - units
        down_terms_ref[...] = jnp.concatenate([down, jnp.zeros((block, empty), BF16)], axis=1)


def lane_up(count):
    return -(-count // LANES) * LANES


def dense_forward(pieces, coords, gates, ups, downs):
    size = lax.axis_size("tensor")
    wide, tokens = pieces[0][0].shape
    units, half_width = downs[0].shape
    parts = size // 4
    block = parts * wide // 2
    own = lambda i, c: (0, jnp.minimum(i, 1))
    other = lambda i, c: (0, jnp.clip(i - 2, 0, 1))
    whole = lambda shape: pl.BlockSpec(shape, lambda i, c: (0, 0))
    term = lambda lanes: pl.BlockSpec((block, lanes), lambda i, c: (jnp.maximum(i - 4, 0), 0))
    return pl.pallas_call(
        functools.partial(dense_kernel, [piece[1] for piece in pieces]),
        grid_spec=pltpu.PrefetchScalarGridSpec(
            num_scalar_prefetch=1,
            grid=(6,),
            in_specs=[pl.BlockSpec(memory_space=pl.ANY)] * len(pieces)
            + [pl.BlockSpec((units, block), own), pl.BlockSpec((units, block), other)] * 3,
            out_specs=[
                pl.BlockSpec((parts, wide, tokens), lambda i, c: (jnp.minimum(i, 1), 0, 0)),
                whole((2 * units, tokens)),
                whole((units, tokens)),
                term(lane_up(2 * units)),
                term(lane_up(units)),
            ],
            scratch_shapes=[
                pltpu.VMEM((size, wide, tokens), BF16),
                pltpu.SemaphoreType.DMA((size,)),
                pltpu.VMEM((2 * units, tokens), F32),
                pltpu.VMEM((units, tokens), F32),
            ],
        ),
        out_shape=[
            shape_of((2 * parts, wide, tokens)),
            shape_of((2 * units, tokens)),
            shape_of((units, tokens)),
            shape_of((half_width, lane_up(2 * units))),
            shape_of((half_width, lane_up(units))),
        ],
        compiler_params=params(),
        cost_estimate=costs(10),
    )(coords, *[piece[0] for piece in pieces], *gates, *ups, *downs)


def terms_kernel(both_ref, backs_ref, hidden_ref, pair_arrived_ref, down_arrived_ref, terms_ref):
    parts, wide, tokens = both_ref.shape
    feats = wide // 2
    units = hidden_ref.shape[0]
    block = parts * feats
    first = pair_arrived_ref.shape[1]
    rows_in = both_ref[:, :feats, :].reshape(block, tokens)
    rows_out = both_ref[:, feats:, :].reshape(block, tokens)
    backs = contract(rows_in, backs_ref[...], 1, 1) + pair_arrived_ref[:, : 2 * units].astype(F32)
    down = contract(rows_out, hidden_ref[...], 1, 1) + down_arrived_ref[:, :units].astype(F32)
    empty = jnp.zeros((block, first - 2 * units), BF16)
    terms_ref[:, :first] = jnp.concatenate([backs.astype(BF16), empty], axis=1)
    empty = jnp.zeros((block, terms_ref.shape[1] - first - units), BF16)
    terms_ref[:, first:] = jnp.concatenate([down.astype(BF16), empty], axis=1)


def dense_terms(own, backs, hidden, pair_arrived, down_arrived):
    size, wide, tokens = own.shape
    units = hidden.shape[0]
    parts = size // 2
    block = parts * wide // 2
    half_width, first = pair_arrived.shape
    second = down_arrived.shape[1]
    whole = lambda shape: pl.BlockSpec(shape, lambda i: (0, 0))
    tall = lambda lanes: pl.BlockSpec((block, lanes), lambda i: (i, 0))
    return pl.pallas_call(
        terms_kernel,
        grid=(2,),
        in_specs=[
            pl.BlockSpec((parts, wide, tokens), lambda i: (i, 0, 0)),
            whole((2 * units, tokens)),
            whole((units, tokens)),
            tall(first),
            tall(second),
        ],
        out_specs=tall(first + second),
        out_shape=shape_of((half_width, first + second)),
        compiler_params=params(),
        cost_estimate=costs(5),
    )(own, backs, hidden, pair_arrived, down_arrived)


def expert_kernel(
    capacity,
    coords_ref,
    slices_ref,
    gate_own_ref,
    gate_other_ref,
    up_own_ref,
    up_other_ref,
    down_own_ref,
    down_other_ref,
    rows_in_ref,
    scaled_out_ref,
    sent_ref,
    hidden_ref,
    backs_ref,
    pre,
    from_down,
    folded,
    scale,
):
    step = pl.program_id(0)
    quarters = pl.num_programs(0) // 2
    pair, main, _ = slices_ref.shape
    block = gate_own_ref.shape[1]
    units = hidden_ref.shape[1]
    feats = block // pair
    piece = feats * 2 // quarters
    rest = rows_in_ref.shape[0] - main
    left = capacity - TILE
    owned = lax.rem(step, quarters) < quarters // 2
    place = lax.rem(coords_ref[1] * (quarters // 2) + step, quarters)

    source = lax.broadcasted_iota(jnp.int32, (main, rest), 1)
    target = lax.broadcasted_iota(jnp.int32, (main, rest), 0)

    def fold(quarter):
        return select(target == source // left * TILE + quarter * left + source % left)

    @pl.when(step == 0)
    def _():
        pre[...] = jnp.zeros_like(pre)
        from_down[...] = jnp.zeros_like(from_down)
        folded[...] = jnp.zeros_like(folded)

    def forward(gate_ref, up_ref, down_ref):
        pair_rows = jnp.concatenate([gate_ref[...], up_ref[...]], axis=0)
        parts = [slices_ref[part] for part in range(pair)]

        @pl.when(step == 0)
        def _():
            scales = parts[0][:, 2 * feats + piece :]
            scale[:main] = scales[:, 0:1].astype(F32)
            scale[main:] = contract(fold(0), scales, 0, 0)[:, 1:2]

        rows_in_ref[:main] = jnp.concatenate([part[:, :feats] for part in parts], axis=1)
        rows_out = jnp.concatenate([part[:, feats : 2 * feats] for part in parts], axis=1)
        beside = jnp.concatenate(
            [part[:, 2 * feats : 2 * feats + piece] for part in parts], axis=1
        )
        spread = [contract(fold(quarter), beside, 0, 0).astype(BF16) for quarter in range(quarters)]
        half = quarters // 2

        def unfolded(which):
            return jnp.concatenate(
                [
                    spread[which * half + quarter][:, part * piece : (part + 1) * piece]
                    for part in range(pair)
                    for quarter in range(half)
                ],
                axis=1,
            )

        rows_in_ref[main:] = unfolded(0)
        rows_out = jnp.concatenate([rows_out, unfolded(1)], axis=0)
        scaled_out_ref[...] = (scale[...] * rows_out.astype(F32)).astype(BF16)
        pre[...] += contract(rows_in_ref[...], pair_rows, 1, 1)
        from_down[...] += contract(rows_out, down_ref[...], 1, 1)

    @pl.when((step < quarters) & owned)
    def _():
        forward(gate_own_ref, up_own_ref, down_own_ref)

    @pl.when((step < quarters) & jnp.logical_not(owned))
    def _():
        forward(gate_other_ref, up_other_ref, down_other_ref)

    @pl.when(step == quarters - 1)
    def _():
        back = from_down[...]
        act, slope = sigmoid_parts(pre[:, :units])
        raised = pre[:, units:]
        hidden = (act * raised).astype(BF16)
        hidden_ref[...] = hidden
        scaled = scale[...] * back
        backs_ref[...] = jnp.concatenate(
            [(scaled * raised * slope).astype(BF16), (scaled * act).astype(BF16)], axis=1
        )
        probe = jnp.sum(hidden.astype(F32) * back, axis=1, keepdims=True)
        high = probe.astype(BF16).astype(F32)
        low = probe - high
        lane = lax.broadcasted_iota(jnp.int32, (main, LANES), 1)
        beside = jnp.where(lane == 0, high[:main], jnp.where(lane == 1, low[:main], 0.0))
        lane = lax.broadcasted_iota(jnp.int32, (rest, LANES), 1)
        after = jnp.where(lane == 2, high[main:], jnp.where(lane == 3, low[main:], 0.0))
        after = jnp.dot(fold(0), after.astype(BF16), preferred_element_type=F32)
        sent_ref[:, sent_ref.shape[1] - LANES :] = (beside + after).astype(BF16)

    def backward(gate_ref, up_ref):
        pair_rows = jnp.concatenate([gate_ref[...], up_ref[...]], axis=0)
        rows = jnp.dot(backs_ref[...], pair_rows, preferred_element_type=F32).astype(BF16)
        sent_ref[:, pl.ds(pl.multiple_of(place * block, LANES), block)] = rows[:main]
        folded[...] += jnp.dot(fold(place), rows[main:], preferred_element_type=F32)

    @pl.when((step >= quarters) & owned)
    def _():
        backward(gate_own_ref, up_own_ref)

    @pl.when((step >= quarters) & jnp.logical_not(owned))
    def _():
        backward(gate_other_ref, up_other_ref)

    @pl.when(step == 2 * quarters - 1)
    def _():
        sent_ref[:, quarters * block : (quarters + 1) * block] = folded[...].astype(BF16)


def expert_rows(slices, coords, gates, ups, downs, experts, capacity):
    size, main, wide = slices.shape
    units, half_width = downs[0].shape
    width = 2 * half_width
    quarters = TILE // (capacity - TILE)
    block = width // quarters
    rows = experts * capacity
    whole = lambda shape: pl.BlockSpec(shape, lambda i, c: (0, 0))
    last = quarters // 2 - 1

    def early(i, c):
        return (0, lax.rem(c[1] * (quarters // 2) + jnp.minimum(i, quarters - 1), quarters))

    def own(i, c):
        return (0, jnp.minimum(lax.rem(i, quarters), last))

    def other(i, c):
        return (0, jnp.maximum(lax.rem(i, quarters), last + 1) - last - 1)

    def own_once(i, c):
        return (0, jnp.minimum(i, last))

    def other_once(i, c):
        return (0, jnp.clip(i - last - 1, 0, last))

    return pl.pallas_call(
        functools.partial(expert_kernel, capacity),
        grid_spec=pltpu.PrefetchScalarGridSpec(
            num_scalar_prefetch=1,
            grid=(2 * quarters,),
            in_specs=[pl.BlockSpec((size // quarters, main, wide), lambda i, c: early(i, c)[::-1] + (0,))]
            + [pl.BlockSpec((units, block), own), pl.BlockSpec((units, block), other)] * 2
            + [pl.BlockSpec((units, block), own_once), pl.BlockSpec((units, block), other_once)],
            out_specs=[
                pl.BlockSpec((rows, block), early),
                pl.BlockSpec((rows, block), early),
                whole((main, width + block + LANES)),
                whole((rows, units)),
                whole((rows, 2 * units)),
            ],
            scratch_shapes=[
                pltpu.VMEM((rows, 2 * units), F32),
                pltpu.VMEM((rows, units), F32),
                pltpu.VMEM((main, block), F32),
                pltpu.VMEM((rows, 1), F32),
            ],
        ),
        out_shape=[
            shape_of((rows, width)),
            shape_of((rows, width)),
            shape_of((main, width + block + LANES)),
            shape_of((rows, units)),
            shape_of((rows, 2 * units)),
        ],
        compiler_params=params(),
        cost_estimate=costs(16),
    )(coords, slices, *gates, *ups, *downs)


def combine_kernel(
    left,
    coords_ref,
    main_ref,
    folded_ref,
    probe_ref,
    places_ref,
    dense_own_ref,
    dense_other_ref,
    total_ref,
):
    step = pl.program_id(0)
    quarters = pl.num_programs(0)
    quarter = lax.rem(coords_ref[1] * (quarters // 2) + step, quarters)
    slots = main_ref.shape[0]
    parts, tall, tokens = total_ref.shape
    feats = tall - TILE
    lane = lax.broadcasted_iota(jnp.int32, (tokens, slots), 1)
    down = (((0,), (1,)), ((), ()))
    pick = lambda place: jnp.where(lane == place, 1.0, 0.0).astype(BF16)
    first = [pick(places_ref[:, k : k + 1]) for k in range(TOP)]
    shifted = [pick(places_ref[:, TOP + k : TOP + k + 1] + quarter * left) for k in range(TOP)]
    rows = lax.dot_general(
        main_ref[...], first[0] + first[1], down, preferred_element_type=F32
    ) + lax.dot_general(
        folded_ref[...], shifted[0] + shifted[1], down, preferred_element_type=F32
    )
    dense = jnp.where(step < quarters // 2, dense_own_ref[...], dense_other_ref[...])
    rows = (dense + rows).astype(BF16)
    for part in range(parts):
        total_ref[part, :feats, :] = rows[part * feats : (part + 1) * feats]
    probes = []
    for k in range(TOP):
        near = lax.dot_general(probe_ref[...], first[k], down, preferred_element_type=F32)
        far = pick(places_ref[:, TOP + k : TOP + k + 1])
        far = lax.dot_general(probe_ref[...], far, down, preferred_element_type=F32)
        probes.append(near[0:1] + near[1:2] + (far[2:3] + far[3:4]))
    probes = jnp.concatenate(probes, axis=0)
    high = probes.astype(BF16).astype(F32)
    empty = jnp.zeros((TILE - 2 * TOP, tokens), F32)
    extra = jnp.concatenate([high, probes - high, empty], axis=0).astype(BF16)
    for part in range(parts):
        total_ref[part, feats:, :] = extra


def combine(back, coords, places, dense_own, dense_other, size, capacity):
    half_width, tokens = dense_own.shape
    width = 2 * half_width
    left = capacity - TILE
    quarters = TILE // left
    block = width // quarters
    slots = back.shape[0]
    feats = width // size
    last = quarters // 2 - 1
    return pl.pallas_call(
        functools.partial(combine_kernel, left),
        grid_spec=pltpu.PrefetchScalarGridSpec(
            num_scalar_prefetch=1,
            grid=(quarters,),
            in_specs=[
                pl.BlockSpec(
                    (slots, block), lambda i, c: (0, lax.rem(c[1] * (quarters // 2) + i, quarters))
                ),
                pl.BlockSpec((slots, block), lambda i, c: (0, quarters)),
                pl.BlockSpec((slots, LANES), lambda i, c: (0, (quarters + 1) * block // LANES)),
                pl.BlockSpec((tokens, 2 * TOP), lambda i, c: (0, 0)),
                pl.BlockSpec((block, tokens), lambda i, c: (jnp.minimum(i, last), 0)),
                pl.BlockSpec((block, tokens), lambda i, c: (jnp.maximum(i, last + 1) - last - 1, 0)),
            ],
            out_specs=pl.BlockSpec(
                (size // quarters, feats + TILE, tokens),
                lambda i, c: (lax.rem(c[1] * (quarters // 2) + i, quarters), 0, 0),
            ),
        ),
        out_shape=jax.ShapeDtypeStruct((size, feats + TILE, tokens), BF16),
        compiler_params=pltpu.CompilerParams(
            dimension_semantics=("arbitrary",), vmem_limit_bytes=VMEM_LIMIT
        ),
        cost_estimate=costs(6),
    )(coords, back, back, back, places, dense_own, dense_other)


def local(
    layer_input,
    cotangent,
    route_probs,
    routes,
    shared_gate,
    shared_up,
    shared_down,
    routed_gate,
    routed_up,
    routed_down,
):
    tok_rows, feats = layer_input.shape
    experts = lax.axis_size("expert")
    capacity = 5 * TOP * tok_rows // (4 * experts)

    both = jnp.concatenate([layer_input.T, cotangent.T], axis=0)
    coords = jnp.stack([lax.axis_index("tensor"), lax.axis_index("dp")]).astype(jnp.int32)

    def with_other(own):
        return own, swap(own)

    dense_weights = [
        with_other(weight) for weight in (shared_gate.T, shared_up.T, shared_down)
    ]
    expert_weights = [
        with_other(weight) for weight in (routed_gate[0].T, routed_up[0].T, routed_down[0])
    ]

    folded, places = dispatch(routes.T, route_probs.T, both, experts, capacity)
    size = lax.axis_size("tensor")
    arrived = lax.all_to_all(
        folded.reshape(experts, TILE, -1), "expert", split_axis=0, concat_axis=0, tiled=True
    )
    pieces = single_ring(both, range(1, size // 2 + 1))[0] + [(both, 0)]
    distances = [piece[1] for piece in pieces]
    arrived, pieces, dense_weights = lax.optimization_barrier(
        (arrived, [piece[0] for piece in pieces], dense_weights)
    )
    pieces = list(zip(pieces, distances))
    slices = lax.all_gather(
        arrived.reshape(experts * TILE, -1), "tensor", axis=0, tiled=False
    )

    own_rows, dense_backs, dense_hidden, pair_terms, down_terms = dense_forward(
        pieces, coords, *dense_weights
    )
    terms = dense_terms(own_rows, dense_backs, dense_hidden, swap(pair_terms), swap(down_terms))
    terms = terms.reshape(experts, -1, terms.shape[1])
    terms = lax.all_to_all(terms, "expert", split_axis=0, concat_axis=0, tiled=True)
    units = dense_hidden.shape[0]
    dense_own, dense_other = [
        product("hd,hn->dn", gate, dense_backs[:units])
        + product("hd,hn->dn", up, dense_backs[units:])
        for gate, up in zip(*dense_weights[:2])
    ]

    slot_in, scaled_out, sent, hidden, backs = expert_rows(
        slices, coords, *expert_weights, experts, capacity
    )
    sent, terms = lax.optimization_barrier((sent, terms))
    terms = terms.astype(F32).sum(axis=0).astype(BF16)
    first = lane_up(2 * units)
    grad_gate = terms[:, :units]
    grad_up = terms[:, units : 2 * units]
    grad_down = terms[:, first : first + units].T
    back = lax.all_to_all(
        sent.reshape(experts, TILE, -1), "expert", split_axis=0, concat_axis=0, tiled=True
    )

    def reduced(rows, backs):
        own, other = halves(rows, 1)
        arrived = swap(product("sh,sd->hd", backs, other).astype(BF16))
        return (product("sh,sd->hd", backs, own) + arrived.astype(F32)).astype(BF16)

    delta_pair = reduced(slot_in, backs)
    delta_gate = delta_pair[:units].T[None]
    delta_up = delta_pair[units:].T[None]
    delta_down = reduced(scaled_out, hidden)[None]

    total = combine(
        back.reshape(experts * TILE, -1),
        coords,
        places,
        dense_own,
        dense_other,
        lax.axis_size("tensor"),
        capacity,
    )
    total = lax.all_to_all(total, "tensor", split_axis=0, concat_axis=0, tiled=True)
    total = total.astype(F32).sum(axis=0)
    input_grad = total[:feats].T.astype(BF16)
    prob_grad = (total[feats : feats + TOP] + total[feats + TOP : feats + 2 * TOP]).T
    return (
        input_grad,
        prob_grad,
        grad_gate,
        grad_up,
        grad_down,
        delta_gate,
        delta_up,
        delta_down,
    )


def solution(mesh):
    return jax.shard_map(
        local,
        mesh=mesh,
        in_specs=(
            P(("dp", "expert"), "tensor"),
            P(("dp", "expert"), "tensor"),
            P(("dp", "expert"), None),
            P(("dp", "expert"), None),
            P("dp", "tensor"),
            P("dp", "tensor"),
            P("tensor", "dp"),
            P("expert", "dp", "tensor"),
            P("expert", "dp", "tensor"),
            P("expert", "tensor", "dp"),
        ),
        out_specs=(
            P(("dp", "expert"), "tensor"),
            P(("dp", "expert"), None),
            P(("dp", "expert"), "tensor"),
            P(("dp", "expert"), "tensor"),
            P("tensor", ("dp", "expert")),
            P("expert", "dp", "tensor"),
            P("expert", "dp", "tensor"),
            P("expert", "tensor", "dp"),
        ),
        check_vma=False,
    )
```

```python
import functools

import jax
import jax.numpy as jnp
from jax import lax
from jax.experimental import pallas as pl
from jax.experimental.pallas import tpu as pltpu
from jax.sharding import PartitionSpec as P

TOP = 2
TILE = 16
LANES = 128
VMEM_LIMIT = 56 * 1024 * 1024
F32 = jnp.float32
BF16 = jnp.bfloat16


def product(spec, left, right):
    return jnp.einsum(spec, left, right, preferred_element_type=F32)


def swap(values):
    return lax.ppermute(values, "dp", [(0, 1), (1, 0)])


def ring(values, shift):
    size = lax.axis_size("tensor")
    return lax.ppermute(values, "tensor", [(i, (i + shift) % size) for i in range(size)])


def single_ring(chunk, steps, state=None):
    size = lax.axis_size("tensor")
    right, left = state or (chunk, chunk)
    pieces = []
    for step in steps:
        right = ring(right, 1)
        pieces.append((right, size - step))
        if step < size - step:
            left = ring(left, -1)
            pieces.append((left, step))
    return pieces, (right, left)


def halves(values, axis):
    half = values.shape[axis] // 2
    index = lax.axis_index("dp")
    return (
        lax.dynamic_slice_in_dim(values, index * half, half, axis),
        lax.dynamic_slice_in_dim(values, (1 - index) * half, half, axis),
    )


def sigmoid_parts(pre_gate):
    sigmoid = 1.0 / (1.0 + jnp.exp(jnp.minimum(-pre_gate, 80.0)))
    return pre_gate * sigmoid, sigmoid * (1.0 + pre_gate * (1.0 - sigmoid))


def select(mask):
    return jnp.where(mask, 1.0, 0.0).astype(BF16)


def contract(left, right, left_dim, right_dim):
    return lax.dot_general(
        left, right, (((left_dim,), (right_dim,)), ((), ())), preferred_element_type=F32
    )


def costs(micros):
    return pl.CostEstimate(flops=1, bytes_accessed=int(micros * 3.5e6), transcendentals=0)


def shape_of(shape, dtype=BF16):
    return jax.ShapeDtypeStruct(shape, dtype)


def params():
    return pltpu.CompilerParams(
        dimension_semantics=("arbitrary",), vmem_limit_bytes=VMEM_LIMIT
    )


def dispatch_kernel(capacity, routes_ref, probs_ref, both_ref, folded_ref, places_ref):
    tokens = routes_ref.shape[1]
    main, wide = folded_ref.shape
    feats = both_ref.shape[0]
    left = capacity - TILE
    quarters = TILE // left
    piece = feats // quarters
    lane = lax.broadcasted_iota(jnp.int32, (tokens, LANES), 1)
    row = lax.broadcasted_iota(jnp.int32, (tokens, tokens), 0)
    column = lax.broadcasted_iota(jnp.int32, (tokens, tokens), 1)

    def column_of(ref, k):
        return jnp.broadcast_to(ref[k : k + 1, :].astype(F32), (tokens, tokens)).T

    routed = [column_of(routes_ref, k).astype(jnp.int32) for k in range(TOP)]
    probs = [column_of(probs_ref, k).astype(BF16).astype(F32)[:, :LANES] for k in range(TOP)]
    named = [lane == routed[k][:, :LANES] for k in range(TOP)]
    earlier = jnp.dot(
        select(row > column), select(named[0] | named[1]), preferred_element_type=F32
    )
    slot = lax.broadcasted_iota(jnp.int32, (tokens, main), 1)
    near, far = [], []
    for k in range(TOP):
        rank = jnp.sum(jnp.where(named[k], earlier, 0.0), axis=1, keepdims=True).astype(jnp.int32)
        first = routed[k][:, :1] * TILE + rank
        near.append(jnp.where(rank < TILE, first, -main))
        far.append(jnp.where(rank < TILE, -main, first - TILE))
    for k in range(TOP):
        places_ref[:, k : k + 1] = near[k]
        places_ref[:, TOP + k : TOP + k + 1] = far[k]
    near = [select(slot == place) for place in near]
    folded_ref[:, :feats] = contract(near[0] + near[1], both_ref[...], 0, 1).astype(BF16)
    rest = jnp.zeros((main, piece), F32)
    for quarter in range(quarters):
        picked = [select(slot == place + quarter * left) for place in far]
        rest += contract(
            picked[0] + picked[1], both_ref[quarter * piece : (quarter + 1) * piece, :], 0, 1
        )
    folded_ref[:, feats : feats + piece] = rest.astype(BF16)
    scales = jnp.zeros((main, LANES), F32)
    for k in range(TOP):
        scales += contract(near[k], jnp.where(lane == 0, probs[k], 0.0).astype(BF16), 0, 0)
        scales += contract(
            select(slot == far[k]), jnp.where(lane == 1, probs[k], 0.0).astype(BF16), 0, 0
        )
    folded_ref[:, feats + piece :] = scales[:, : wide - feats - piece].astype(BF16)


def dispatch(routes, probs, both, experts, capacity):
    feats, tokens = both.shape
    wide = feats + feats * (capacity - TILE) // TILE
    wide = (wide // LANES + 1) * LANES
    return pl.pallas_call(
        functools.partial(dispatch_kernel, capacity),
        out_shape=[
            shape_of((experts * TILE, wide)),
            shape_of((tokens, 2 * TOP), jnp.int32),
        ],
        compiler_params=pltpu.CompilerParams(vmem_limit_bytes=VMEM_LIMIT),
        cost_estimate=costs(3),
    )(routes, probs, both)


def dense_kernel(distances, coords_ref, *refs):
    pieces = refs[: len(distances)]
    (
        gate_own_ref,
        gate_other_ref,
        up_own_ref,
        up_other_ref,
        down_own_ref,
        down_other_ref,
        own_ref,
        other_ref,
        backs_ref,
        hidden_ref,
        rows,
        arrivals,
        pre,
        from_down,
    ) = refs[len(distances) :]
    step = pl.program_id(0)
    size, wide, tokens = rows.shape
    parts = size // 4
    feats = wide // 2
    units = hidden_ref.shape[0]
    block = parts * feats
    place = lax.rem(coords_ref[1] * 2 + step, 4)

    @pl.when(step == 0)
    def _():
        for ref, distance in zip(pieces, distances):
            origin = lax.rem(coords_ref[0] + distance, size)
            pltpu.make_async_copy(ref, rows.at[origin], arrivals.at[origin]).start()
        pre[...] = jnp.zeros_like(pre)
        from_down[...] = jnp.zeros_like(from_down)

    for part in range(parts):
        origin = place * parts + part
        pltpu.make_async_copy(pieces[0], rows.at[origin], arrivals.at[origin]).wait()

    @pl.when(step < 2)
    def _():
        own_ref[...] = rows[pl.ds(place * parts, parts)]

    @pl.when(step >= 2)
    def _():
        other_ref[...] = rows[pl.ds(place * parts, parts)]

    rows_in = rows[pl.ds(place * parts, parts), :feats, :].reshape(block, tokens)
    rows_out = rows[pl.ds(place * parts, parts), feats:, :].reshape(block, tokens)

    def forward(gate_ref, up_ref, down_ref):
        pair = jnp.concatenate([gate_ref[...], up_ref[...]], axis=0)
        pre[...] += jnp.dot(pair, rows_in, preferred_element_type=F32)
        from_down[...] += jnp.dot(down_ref[...], rows_out, preferred_element_type=F32)

    @pl.when(step < 2)
    def _():
        forward(gate_own_ref, up_own_ref, down_own_ref)

    @pl.when(step >= 2)
    def _():
        forward(gate_other_ref, up_other_ref, down_other_ref)

    @pl.when(step == 3)
    def _():
        act, slope = sigmoid_parts(pre[:units])
        raised = pre[units:]
        back = from_down[...]
        hidden_ref[...] = (act * raised).astype(BF16)
        backs_ref[:units] = (back * raised * slope).astype(BF16)
        backs_ref[units:] = (back * act).astype(BF16)


def dense_forward(pieces, coords, gates, ups, downs):
    size = lax.axis_size("tensor")
    wide, tokens = pieces[0][0].shape
    units, half_width = downs[0].shape
    parts = size // 4
    block = parts * wide // 2
    own = lambda i, c: (0, jnp.minimum(i, 1))
    other = lambda i, c: (0, jnp.clip(i - 2, 0, 1))
    whole = lambda shape: pl.BlockSpec(shape, lambda i, c: (0, 0))
    return pl.pallas_call(
        functools.partial(dense_kernel, [piece[1] for piece in pieces]),
        grid_spec=pltpu.PrefetchScalarGridSpec(
            num_scalar_prefetch=1,
            grid=(4,),
            in_specs=[pl.BlockSpec(memory_space=pl.ANY)] * len(pieces)
            + [pl.BlockSpec((units, block), own), pl.BlockSpec((units, block), other)] * 3,
            out_specs=[
                pl.BlockSpec((parts, wide, tokens), lambda i, c: (jnp.minimum(i, 1), 0, 0)),
                pl.BlockSpec((parts, wide, tokens), lambda i, c: (jnp.maximum(i - 2, 0), 0, 0)),
                whole((2 * units, tokens)),
                whole((units, tokens)),
            ],
            scratch_shapes=[
                pltpu.VMEM((size, wide, tokens), BF16),
                pltpu.SemaphoreType.DMA((size,)),
                pltpu.VMEM((2 * units, tokens), F32),
                pltpu.VMEM((units, tokens), F32),
            ],
        ),
        out_shape=[
            shape_of((2 * parts, wide, tokens)),
            shape_of((2 * parts, wide, tokens)),
            shape_of((2 * units, tokens)),
            shape_of((units, tokens)),
        ],
        compiler_params=params(),
        cost_estimate=costs(7),
    )(coords, *[piece[0] for piece in pieces], *gates, *ups, *downs)


def terms_kernel(
    own_ref, arrived_ref, backs_ref, backs_arrived_ref, hidden_ref, hidden_arrived_ref, terms_ref
):
    parts, wide, tokens = own_ref.shape
    feats = wide // 2
    units = hidden_ref.shape[0]
    block = parts * feats
    strips = terms_ref.shape[0]
    tall = block // strips
    tiles, tail = 3 * units // LANES, 3 * units % LANES

    def both_blocks(left, right):
        return jnp.concatenate([left, right], axis=1)

    rows_in = both_blocks(
        own_ref[:, :feats, :].reshape(block, tokens), arrived_ref[:, :feats, :].reshape(block, tokens)
    )
    rows_out = both_blocks(
        own_ref[:, feats:, :].reshape(block, tokens), arrived_ref[:, feats:, :].reshape(block, tokens)
    )
    backs = both_blocks(backs_ref[...], backs_arrived_ref[...])
    hidden = both_blocks(hidden_ref[...], hidden_arrived_ref[...])
    terms = jnp.concatenate(
        [contract(rows_in, backs, 1, 1).astype(BF16), contract(rows_out, hidden, 1, 1).astype(BF16)],
        axis=1,
    )
    last = contract(hidden[units - tail :], rows_out, 1, 1).astype(BF16)
    for strip in range(strips):
        rows = slice(strip * tall, (strip + 1) * tall)
        for tile in range(tiles):
            terms_ref[strip, tile * tall : (tile + 1) * tall, :] = terms[
                rows, tile * LANES : (tile + 1) * LANES
            ]
        terms_ref[strip, tiles * tall :, :] = jnp.concatenate(
            [last[:, rows], jnp.zeros((tail, LANES - tall), BF16)], axis=1
        )


def dense_terms(own, arrived, backs, backs_arrived, hidden, hidden_arrived, experts):
    size, wide, tokens = own.shape
    units = hidden.shape[0]
    parts = size // 2
    tall = size * wide // 2 // experts
    deep = 3 * units // LANES * tall + 3 * units % LANES
    whole = lambda shape: pl.BlockSpec(shape, lambda i: (0, 0))
    rows = pl.BlockSpec((parts, wide, tokens), lambda i: (i, 0, 0))
    return pl.pallas_call(
        terms_kernel,
        grid=(2,),
        in_specs=[rows] * 2 + [whole((2 * units, tokens))] * 2 + [whole((units, tokens))] * 2,
        out_specs=pl.BlockSpec((experts // 2, deep, LANES), lambda i: (i, 0, 0)),
        out_shape=shape_of((experts, deep, LANES)),
        compiler_params=params(),
        cost_estimate=costs(5),
    )(own, arrived, backs, backs_arrived, hidden, hidden_arrived)


def unpacked(terms, units, tall):
    tiles, tail = 3 * units // LANES, 3 * units % LANES
    whole = terms[: tiles * tall].reshape(tiles, tall, LANES).transpose(1, 0, 2)
    return jnp.concatenate(
        [whole.reshape(tall, tiles * LANES), terms[tiles * tall :, :tall].T], axis=1
    )


def expert_kernel(
    capacity,
    coords_ref,
    slices_ref,
    gate_own_ref,
    gate_other_ref,
    up_own_ref,
    up_other_ref,
    down_own_ref,
    down_other_ref,
    rows_in_ref,
    scaled_out_ref,
    sent_ref,
    hidden_ref,
    backs_ref,
    pre,
    from_down,
    folded,
    scale,
):
    step = pl.program_id(0)
    quarters = pl.num_programs(0) // 2
    pair, main, _ = slices_ref.shape
    block = gate_own_ref.shape[1]
    units = hidden_ref.shape[1]
    feats = block // pair
    piece = feats * 2 // quarters
    rest = rows_in_ref.shape[0] - main
    left = capacity - TILE
    owned = lax.rem(step, quarters) < quarters // 2
    place = lax.rem(coords_ref[1] * (quarters // 2) + step, quarters)

    source = lax.broadcasted_iota(jnp.int32, (main, rest), 1)
    target = lax.broadcasted_iota(jnp.int32, (main, rest), 0)

    def fold(quarter):
        return select(target == source // left * TILE + quarter * left + source % left)

    @pl.when(step == 0)
    def _():
        pre[...] = jnp.zeros_like(pre)
        from_down[...] = jnp.zeros_like(from_down)
        folded[...] = jnp.zeros_like(folded)

    def forward(gate_ref, up_ref, down_ref):
        pair_rows = jnp.concatenate([gate_ref[...], up_ref[...]], axis=0)
        parts = [slices_ref[part] for part in range(pair)]

        @pl.when(step == 0)
        def _():
            scales = parts[0][:, 2 * feats + piece :]
            scale[:main] = scales[:, 0:1].astype(F32)
            scale[main:] = contract(fold(0), scales, 0, 0)[:, 1:2]

        rows_in_ref[:main] = jnp.concatenate([part[:, :feats] for part in parts], axis=1)
        rows_out = jnp.concatenate([part[:, feats : 2 * feats] for part in parts], axis=1)
        beside = jnp.concatenate(
            [part[:, 2 * feats : 2 * feats + piece] for part in parts], axis=1
        )
        spread = [contract(fold(quarter), beside, 0, 0).astype(BF16) for quarter in range(quarters)]
        half = quarters // 2

        def unfolded(which):
            return jnp.concatenate(
                [
                    spread[which * half + quarter][:, part * piece : (part + 1) * piece]
                    for part in range(pair)
                    for quarter in range(half)
                ],
                axis=1,
            )

        rows_in_ref[main:] = unfolded(0)
        rows_out = jnp.concatenate([rows_out, unfolded(1)], axis=0)
        scaled_out_ref[...] = (scale[...] * rows_out.astype(F32)).astype(BF16)
        pre[...] += contract(rows_in_ref[...], pair_rows, 1, 1)
        from_down[...] += contract(rows_out, down_ref[...], 1, 1)

    @pl.when((step < quarters) & owned)
    def _():
        forward(gate_own_ref, up_own_ref, down_own_ref)

    @pl.when((step < quarters) & jnp.logical_not(owned))
    def _():
        forward(gate_other_ref, up_other_ref, down_other_ref)

    @pl.when(step == quarters - 1)
    def _():
        back = from_down[...]
        act, slope = sigmoid_parts(pre[:, :units])
        raised = pre[:, units:]
        hidden = (act * raised).astype(BF16)
        hidden_ref[...] = hidden
        scaled = scale[...] * back
        backs_ref[...] = jnp.concatenate(
            [(scaled * raised * slope).astype(BF16), (scaled * act).astype(BF16)], axis=1
        )
        probe = jnp.sum(hidden.astype(F32) * back, axis=1, keepdims=True)
        high = probe.astype(BF16).astype(F32)
        low = probe - high
        lane = lax.broadcasted_iota(jnp.int32, (main, LANES), 1)
        beside = jnp.where(lane == 0, high[:main], jnp.where(lane == 1, low[:main], 0.0))
        lane = lax.broadcasted_iota(jnp.int32, (rest, LANES), 1)
        after = jnp.where(lane == 2, high[main:], jnp.where(lane == 3, low[main:], 0.0))
        after = jnp.dot(fold(0), after.astype(BF16), preferred_element_type=F32)
        sent_ref[:, sent_ref.shape[1] - LANES :] = (beside + after).astype(BF16)

    def backward(gate_ref, up_ref):
        pair_rows = jnp.concatenate([gate_ref[...], up_ref[...]], axis=0)
        rows = jnp.dot(backs_ref[...], pair_rows, preferred_element_type=F32).astype(BF16)
        sent_ref[:, pl.ds(pl.multiple_of(place * block, LANES), block)] = rows[:main]
        folded[...] += jnp.dot(fold(place), rows[main:], preferred_element_type=F32)

    @pl.when((step >= quarters) & owned)
    def _():
        backward(gate_own_ref, up_own_ref)

    @pl.when((step >= quarters) & jnp.logical_not(owned))
    def _():
        backward(gate_other_ref, up_other_ref)

    @pl.when(step == 2 * quarters - 1)
    def _():
        sent_ref[:, quarters * block : (quarters + 1) * block] = folded[...].astype(BF16)


def expert_rows(slices, coords, gates, ups, downs, experts, capacity):
    size, main, wide = slices.shape
    units, half_width = downs[0].shape
    width = 2 * half_width
    quarters = TILE // (capacity - TILE)
    block = width // quarters
    rows = experts * capacity
    whole = lambda shape: pl.BlockSpec(shape, lambda i, c: (0, 0))
    last = quarters // 2 - 1

    def early(i, c):
        return (0, lax.rem(c[1] * (quarters // 2) + jnp.minimum(i, quarters - 1), quarters))

    def own(i, c):
        return (0, jnp.minimum(lax.rem(i, quarters), last))

    def other(i, c):
        return (0, jnp.maximum(lax.rem(i, quarters), last + 1) - last - 1)

    def own_once(i, c):
        return (0, jnp.minimum(i, last))

    def other_once(i, c):
        return (0, jnp.clip(i - last - 1, 0, last))

    return pl.pallas_call(
        functools.partial(expert_kernel, capacity),
        grid_spec=pltpu.PrefetchScalarGridSpec(
            num_scalar_prefetch=1,
            grid=(2 * quarters,),
            in_specs=[pl.BlockSpec((size // quarters, main, wide), lambda i, c: early(i, c)[::-1] + (0,))]
            + [pl.BlockSpec((units, block), own), pl.BlockSpec((units, block), other)] * 2
            + [pl.BlockSpec((units, block), own_once), pl.BlockSpec((units, block), other_once)],
            out_specs=[
                pl.BlockSpec((rows, block), early),
                pl.BlockSpec((rows, block), early),
                whole((main, width + block + LANES)),
                whole((rows, units)),
                whole((rows, 2 * units)),
            ],
            scratch_shapes=[
                pltpu.VMEM((rows, 2 * units), F32),
                pltpu.VMEM((rows, units), F32),
                pltpu.VMEM((main, block), F32),
                pltpu.VMEM((rows, 1), F32),
            ],
        ),
        out_shape=[
            shape_of((rows, width)),
            shape_of((rows, width)),
            shape_of((main, width + block + LANES)),
            shape_of((rows, units)),
            shape_of((rows, 2 * units)),
        ],
        compiler_params=params(),
        cost_estimate=costs(16),
    )(coords, slices, *gates, *ups, *downs)


def combine_kernel(
    left,
    coords_ref,
    main_ref,
    folded_ref,
    probe_ref,
    places_ref,
    dense_own_ref,
    dense_other_ref,
    total_ref,
    extra,
):
    step = pl.program_id(0)
    quarters = pl.num_programs(0)
    quarter = lax.rem(coords_ref[1] * (quarters // 2) + step, quarters)
    slots = main_ref.shape[0]
    parts, tall, tokens = total_ref.shape
    feats = tall - TILE
    lane = lax.broadcasted_iota(jnp.int32, (tokens, slots), 1)
    pick = lambda place: select(lane == place)
    near = [pick(places_ref[:, k : k + 1]) for k in range(TOP)]
    far = [places_ref[:, TOP + k : TOP + k + 1] for k in range(TOP)]

    @pl.when(step == 0)
    def _():
        probes = []
        for k in range(TOP):
            first = contract(probe_ref[...], near[k], 0, 1)
            second = contract(probe_ref[...], pick(far[k]), 0, 1)
            probes.append(first[0:1] + first[1:2] + (second[2:3] + second[3:4]))
        probes = jnp.concatenate(probes, axis=0)
        high = probes.astype(BF16).astype(F32)
        empty = jnp.zeros((TILE - 2 * TOP, tokens), F32)
        extra[...] = jnp.concatenate([high, probes - high, empty], axis=0).astype(BF16)

    shifted = [pick(place + quarter * left) for place in far]
    rows = jnp.dot(near[0] + near[1], main_ref[...], preferred_element_type=F32)
    rows += jnp.dot(shifted[0] + shifted[1], folded_ref[...], preferred_element_type=F32)
    dense = jnp.where(step < quarters // 2, dense_own_ref[...], dense_other_ref[...])
    rows = (dense + rows.T).astype(BF16)
    for part in range(parts):
        total_ref[part, :feats, :] = rows[part * feats : (part + 1) * feats]
        total_ref[part, feats:, :] = extra[...]


def combine(back, coords, places, dense_own, dense_other, size, capacity):
    half_width, tokens = dense_own.shape
    width = 2 * half_width
    left = capacity - TILE
    quarters = TILE // left
    block = width // quarters
    slots = back.shape[0]
    feats = width // size
    last = quarters // 2 - 1
    return pl.pallas_call(
        functools.partial(combine_kernel, left),
        grid_spec=pltpu.PrefetchScalarGridSpec(
            num_scalar_prefetch=1,
            grid=(quarters,),
            in_specs=[
                pl.BlockSpec(
                    (slots, block), lambda i, c: (0, lax.rem(c[1] * (quarters // 2) + i, quarters))
                ),
                pl.BlockSpec((slots, block), lambda i, c: (0, quarters)),
                pl.BlockSpec((slots, LANES), lambda i, c: (0, (quarters + 1) * block // LANES)),
                pl.BlockSpec((tokens, 2 * TOP), lambda i, c: (0, 0)),
                pl.BlockSpec((block, tokens), lambda i, c: (jnp.minimum(i, last), 0)),
                pl.BlockSpec((block, tokens), lambda i, c: (jnp.maximum(i, last + 1) - last - 1, 0)),
            ],
            out_specs=pl.BlockSpec(
                (size // quarters, feats + TILE, tokens),
                lambda i, c: (lax.rem(c[1] * (quarters // 2) + i, quarters), 0, 0),
            ),
            scratch_shapes=[pltpu.VMEM((TILE, tokens), BF16)],
        ),
        out_shape=jax.ShapeDtypeStruct((size, feats + TILE, tokens), BF16),
        compiler_params=pltpu.CompilerParams(
            dimension_semantics=("arbitrary",), vmem_limit_bytes=VMEM_LIMIT
        ),
        cost_estimate=costs(6),
    )(coords, back, back, back, places, dense_own, dense_other)


def local(
    layer_input,
    cotangent,
    route_probs,
    routes,
    shared_gate,
    shared_up,
    shared_down,
    routed_gate,
    routed_up,
    routed_down,
):
    tok_rows, feats = layer_input.shape
    experts = lax.axis_size("expert")
    capacity = 5 * TOP * tok_rows // (4 * experts)

    both = jnp.concatenate([layer_input.T, cotangent.T], axis=0)
    coords = jnp.stack([lax.axis_index("tensor"), lax.axis_index("dp")]).astype(jnp.int32)

    def with_other(own):
        return own, swap(own)

    dense_weights = [
        with_other(weight) for weight in (shared_gate.T, shared_up.T, shared_down)
    ]
    expert_weights = [
        with_other(weight) for weight in (routed_gate[0].T, routed_up[0].T, routed_down[0])
    ]

    folded, places = dispatch(routes.T, route_probs.T, both, experts, capacity)
    size = lax.axis_size("tensor")
    arrived = lax.all_to_all(
        folded.reshape(experts, TILE, -1), "expert", split_axis=0, concat_axis=0, tiled=True
    )
    pieces, state = single_ring(both, range(1, size // 2))
    arrived, state, dense_weights = lax.optimization_barrier((arrived, state, dense_weights))
    pieces += single_ring(both, [size // 2], state)[0] + [(both, 0)]
    slices = lax.all_gather(
        arrived.reshape(experts * TILE, -1), "tensor", axis=0, tiled=False
    )

    own_rows, other_rows, dense_backs, dense_hidden = dense_forward(
        pieces, coords, *dense_weights
    )
    terms = dense_terms(
        own_rows,
        swap(other_rows),
        dense_backs,
        swap(dense_backs),
        dense_hidden,
        swap(dense_hidden),
        experts,
    )
    terms = lax.all_to_all(terms, "expert", split_axis=0, concat_axis=0, tiled=True)
    units = dense_hidden.shape[0]
    dense_own, dense_other = [
        product("hd,hn->dn", gate, dense_backs[:units])
        + product("hd,hn->dn", up, dense_backs[units:])
        for gate, up in zip(*dense_weights[:2])
    ]

    slot_in, scaled_out, sent, hidden, backs = expert_rows(
        slices, coords, *expert_weights, experts, capacity
    )
    sent, terms = lax.optimization_barrier((sent, terms))
    terms = terms.astype(F32).sum(axis=0).astype(BF16)
    terms = unpacked(terms, units, own_rows.shape[0] * feats // experts)
    grad_gate = terms[:, :units]
    grad_up = terms[:, units : 2 * units]
    grad_down = terms[:, 2 * units :].T
    back = lax.all_to_all(
        sent.reshape(experts, TILE, -1), "expert", split_axis=0, concat_axis=0, tiled=True
    )

    def reduced(rows, backs):
        own, other = halves(rows, 1)
        arrived = swap(product("sh,sd->hd", backs, other).astype(BF16))
        return (product("sh,sd->hd", backs, own) + arrived.astype(F32)).astype(BF16)

    delta_pair = reduced(slot_in, backs)
    delta_gate = delta_pair[:units].T[None]
    delta_up = delta_pair[units:].T[None]
    delta_down = reduced(scaled_out, hidden)[None]

    total = combine(
        back.reshape(experts * TILE, -1),
        coords,
        places,
        dense_own,
        dense_other,
        lax.axis_size("tensor"),
        capacity,
    )
    total = lax.all_to_all(total, "tensor", split_axis=0, concat_axis=0, tiled=True)
    total = total.astype(F32).sum(axis=0)
    input_grad = total[:feats].T.astype(BF16)
    prob_grad = (total[feats : feats + TOP] + total[feats + TOP : feats + 2 * TOP]).T
    return (
        input_grad,
        prob_grad,
        grad_gate,
        grad_up,
        grad_down,
        delta_gate,
        delta_up,
        delta_down,
    )


def solution(mesh):
    return jax.shard_map(
        local,
        mesh=mesh,
        in_specs=(
            P(("dp", "expert"), "tensor"),
            P(("dp", "expert"), "tensor"),
            P(("dp", "expert"), None),
            P(("dp", "expert"), None),
            P("dp", "tensor"),
            P("dp", "tensor"),
            P("tensor", "dp"),
            P("expert", "dp", "tensor"),
            P("expert", "dp", "tensor"),
            P("expert", "tensor", "dp"),
        ),
        out_specs=(
            P(("dp", "expert"), "tensor"),
            P(("dp", "expert"), None),
            P(("dp", "expert"), "tensor"),
            P(("dp", "expert"), "tensor"),
            P("tensor", ("dp", "expert")),
            P("expert", "dp", "tensor"),
            P("expert", "dp", "tensor"),
            P("expert", "tensor", "dp"),
        ),
        check_vma=False,
    )
```

```python
import functools

import jax
import jax.numpy as jnp
from jax import lax
from jax.experimental import pallas as pl
from jax.experimental.pallas import tpu as pltpu
from jax.sharding import PartitionSpec as P

TOP = 2
TILE = 16
LANES = 128
VMEM_LIMIT = 56 * 1024 * 1024
F32 = jnp.float32
BF16 = jnp.bfloat16


def product(spec, left, right):
    return jnp.einsum(spec, left, right, preferred_element_type=F32)


def swap(values):
    return lax.ppermute(values, "dp", [(0, 1), (1, 0)])


def ring(values, shift):
    size = lax.axis_size("tensor")
    return lax.ppermute(values, "tensor", [(i, (i + shift) % size) for i in range(size)])


def single_ring(chunk, steps, state=None):
    size = lax.axis_size("tensor")
    right, left = state or (chunk, chunk)
    pieces = []
    for step in steps:
        right = ring(right, 1)
        pieces.append((right, size - step))
        if step < size - step:
            left = ring(left, -1)
            pieces.append((left, step))
    return pieces, (right, left)


def halves(values, axis):
    half = values.shape[axis] // 2
    index = lax.axis_index("dp")
    return (
        lax.dynamic_slice_in_dim(values, index * half, half, axis),
        lax.dynamic_slice_in_dim(values, (1 - index) * half, half, axis),
    )


def sigmoid_parts(pre_gate):
    sigmoid = 1.0 / (1.0 + jnp.exp(jnp.minimum(-pre_gate, 80.0)))
    return pre_gate * sigmoid, sigmoid * (1.0 + pre_gate * (1.0 - sigmoid))


def select(mask):
    return jnp.where(mask, 1.0, 0.0).astype(BF16)


def contract(left, right, left_dim, right_dim):
    return lax.dot_general(
        left, right, (((left_dim,), (right_dim,)), ((), ())), preferred_element_type=F32
    )


def costs(micros):
    return pl.CostEstimate(flops=1, bytes_accessed=int(micros * 3.5e6), transcendentals=0)


def shape_of(shape, dtype=BF16):
    return jax.ShapeDtypeStruct(shape, dtype)


def params():
    return pltpu.CompilerParams(
        dimension_semantics=("arbitrary",), vmem_limit_bytes=VMEM_LIMIT
    )


def dispatch_kernel(capacity, routes_ref, probs_ref, both_ref, folded_ref, places_ref):
    tokens = routes_ref.shape[1]
    main, wide = folded_ref.shape
    feats = both_ref.shape[0]
    left = capacity - TILE
    quarters = TILE // left
    piece = feats // quarters
    lane = lax.broadcasted_iota(jnp.int32, (tokens, LANES), 1)
    row = lax.broadcasted_iota(jnp.int32, (tokens, tokens), 0)
    column = lax.broadcasted_iota(jnp.int32, (tokens, tokens), 1)

    def column_of(ref, k):
        return jnp.broadcast_to(ref[k : k + 1, :].astype(F32), (tokens, tokens)).T

    routed = [column_of(routes_ref, k).astype(jnp.int32) for k in range(TOP)]
    probs = [column_of(probs_ref, k).astype(BF16).astype(F32)[:, :LANES] for k in range(TOP)]
    named = [lane == routed[k][:, :LANES] for k in range(TOP)]
    earlier = jnp.dot(
        select(row > column), select(named[0] | named[1]), preferred_element_type=F32
    )
    slot = lax.broadcasted_iota(jnp.int32, (tokens, main), 1)
    near, far = [], []
    for k in range(TOP):
        rank = jnp.sum(jnp.where(named[k], earlier, 0.0), axis=1, keepdims=True).astype(jnp.int32)
        first = routed[k][:, :1] * TILE + rank
        near.append(jnp.where(rank < TILE, first, -main))
        far.append(jnp.where(rank < TILE, -main, first - TILE))
    for k in range(TOP):
        places_ref[:, k : k + 1] = near[k]
        places_ref[:, TOP + k : TOP + k + 1] = far[k]
    near = [select(slot == place) for place in near]
    folded_ref[:, :feats] = contract(near[0] + near[1], both_ref[...], 0, 1).astype(BF16)
    rest = jnp.zeros((main, piece), F32)
    for quarter in range(quarters):
        picked = [select(slot == place + quarter * left) for place in far]
        rest += contract(
            picked[0] + picked[1], both_ref[quarter * piece : (quarter + 1) * piece, :], 0, 1
        )
    folded_ref[:, feats : feats + piece] = rest.astype(BF16)
    scales = jnp.zeros((main, LANES), F32)
    for k in range(TOP):
        scales += contract(near[k], jnp.where(lane == 0, probs[k], 0.0).astype(BF16), 0, 0)
        scales += contract(
            select(slot == far[k]), jnp.where(lane == 1, probs[k], 0.0).astype(BF16), 0, 0
        )
    folded_ref[:, feats + piece :] = scales[:, : wide - feats - piece].astype(BF16)


def dispatch(routes, probs, both, experts, capacity):
    feats, tokens = both.shape
    wide = feats + feats * (capacity - TILE) // TILE
    wide = (wide // LANES + 1) * LANES
    return pl.pallas_call(
        functools.partial(dispatch_kernel, capacity),
        out_shape=[
            shape_of((experts * TILE, wide)),
            shape_of((tokens, 2 * TOP), jnp.int32),
        ],
        compiler_params=pltpu.CompilerParams(vmem_limit_bytes=VMEM_LIMIT),
        cost_estimate=costs(3),
    )(routes, probs, both)


def dense_kernel(distances, coords_ref, *refs):
    pieces = refs[: len(distances)]
    (
        gate_own_ref,
        gate_other_ref,
        up_own_ref,
        up_other_ref,
        down_own_ref,
        down_other_ref,
        own_ref,
        other_ref,
        backs_ref,
        hidden_ref,
        rows,
        arrivals,
        pre,
        from_down,
    ) = refs[len(distances) :]
    step = pl.program_id(0)
    size, wide, tokens = rows.shape
    parts = size // 4
    feats = wide // 2
    units = hidden_ref.shape[0]
    block = parts * feats
    place = lax.rem(coords_ref[1] * 2 + step, 4)

    @pl.when(step == 0)
    def _():
        for ref, distance in zip(pieces, distances):
            origin = lax.rem(coords_ref[0] + distance, size)
            pltpu.make_async_copy(ref, rows.at[origin], arrivals.at[origin]).start()
        pre[...] = jnp.zeros_like(pre)
        from_down[...] = jnp.zeros_like(from_down)

    for part in range(parts):
        origin = place * parts + part
        pltpu.make_async_copy(pieces[0], rows.at[origin], arrivals.at[origin]).wait()

    @pl.when(step < 2)
    def _():
        own_ref[...] = rows[pl.ds(place * parts, parts)]

    @pl.when(step >= 2)
    def _():
        other_ref[...] = rows[pl.ds(place * parts, parts)]

    rows_in = rows[pl.ds(place * parts, parts), :feats, :].reshape(block, tokens)
    rows_out = rows[pl.ds(place * parts, parts), feats:, :].reshape(block, tokens)

    def forward(gate_ref, up_ref, down_ref):
        pair = jnp.concatenate([gate_ref[...], up_ref[...]], axis=0)
        pre[...] += jnp.dot(pair, rows_in, preferred_element_type=F32)
        from_down[...] += jnp.dot(down_ref[...], rows_out, preferred_element_type=F32)

    @pl.when(step < 2)
    def _():
        forward(gate_own_ref, up_own_ref, down_own_ref)

    @pl.when(step >= 2)
    def _():
        forward(gate_other_ref, up_other_ref, down_other_ref)

    @pl.when(step == 3)
    def _():
        act, slope = sigmoid_parts(pre[:units])
        raised = pre[units:]
        back = from_down[...]
        hidden_ref[...] = (act * raised).astype(BF16)
        backs_ref[:units] = (back * raised * slope).astype(BF16)
        backs_ref[units:] = (back * act).astype(BF16)


def dense_forward(pieces, coords, gates, ups, downs):
    size = lax.axis_size("tensor")
    wide, tokens = pieces[0][0].shape
    units, half_width = downs[0].shape
    parts = size // 4
    block = parts * wide // 2
    own = lambda i, c: (0, jnp.minimum(i, 1))
    other = lambda i, c: (0, jnp.clip(i - 2, 0, 1))
    whole = lambda shape: pl.BlockSpec(shape, lambda i, c: (0, 0))
    return pl.pallas_call(
        functools.partial(dense_kernel, [piece[1] for piece in pieces]),
        grid_spec=pltpu.PrefetchScalarGridSpec(
            num_scalar_prefetch=1,
            grid=(4,),
            in_specs=[pl.BlockSpec(memory_space=pl.ANY)] * len(pieces)
            + [pl.BlockSpec((units, block), own), pl.BlockSpec((units, block), other)] * 3,
            out_specs=[
                pl.BlockSpec((parts, wide, tokens), lambda i, c: (jnp.minimum(i, 1), 0, 0)),
                pl.BlockSpec((parts, wide, tokens), lambda i, c: (jnp.maximum(i - 2, 0), 0, 0)),
                whole((2 * units, tokens)),
                whole((units, tokens)),
            ],
            scratch_shapes=[
                pltpu.VMEM((size, wide, tokens), BF16),
                pltpu.SemaphoreType.DMA((size,)),
                pltpu.VMEM((2 * units, tokens), F32),
                pltpu.VMEM((units, tokens), F32),
            ],
        ),
        out_shape=[
            shape_of((2 * parts, wide, tokens)),
            shape_of((2 * parts, wide, tokens)),
            shape_of((2 * units, tokens)),
            shape_of((units, tokens)),
        ],
        compiler_params=params(),
        cost_estimate=costs(7),
    )(coords, *[piece[0] for piece in pieces], *gates, *ups, *downs)


def terms_kernel(
    own_ref, arrived_ref, backs_ref, backs_arrived_ref, hidden_ref, hidden_arrived_ref, terms_ref
):
    parts, wide, tokens = own_ref.shape
    feats = wide // 2
    units = hidden_ref.shape[0]
    block = parts * feats
    strips = terms_ref.shape[0]
    tall = block // strips
    tiles, tail = 3 * units // LANES, 3 * units % LANES

    def both_blocks(left, right):
        return jnp.concatenate([left, right], axis=1)

    rows_in = both_blocks(
        own_ref[:, :feats, :].reshape(block, tokens), arrived_ref[:, :feats, :].reshape(block, tokens)
    )
    rows_out = both_blocks(
        own_ref[:, feats:, :].reshape(block, tokens), arrived_ref[:, feats:, :].reshape(block, tokens)
    )
    backs = both_blocks(backs_ref[...], backs_arrived_ref[...])
    hidden = both_blocks(hidden_ref[...], hidden_arrived_ref[...])
    terms = jnp.concatenate(
        [contract(rows_in, backs, 1, 1).astype(BF16), contract(rows_out, hidden, 1, 1).astype(BF16)],
        axis=1,
    )
    last = contract(hidden[units - tail :], rows_out, 1, 1).astype(BF16)
    for strip in range(strips):
        rows = slice(strip * tall, (strip + 1) * tall)
        for tile in range(tiles):
            terms_ref[strip, tile * tall : (tile + 1) * tall, :] = terms[
                rows, tile * LANES : (tile + 1) * LANES
            ]
        terms_ref[strip, tiles * tall :, :] = jnp.concatenate(
            [last[:, rows], jnp.zeros((tail, LANES - tall), BF16)], axis=1
        )


def dense_terms(own, arrived, backs, backs_arrived, hidden, hidden_arrived, experts):
    size, wide, tokens = own.shape
    units = hidden.shape[0]
    parts = size // 2
    tall = size * wide // 2 // experts
    deep = 3 * units // LANES * tall + 3 * units % LANES
    whole = lambda shape: pl.BlockSpec(shape, lambda i: (0, 0))
    rows = pl.BlockSpec((parts, wide, tokens), lambda i: (i, 0, 0))
    return pl.pallas_call(
        terms_kernel,
        grid=(2,),
        in_specs=[rows] * 2 + [whole((2 * units, tokens))] * 2 + [whole((units, tokens))] * 2,
        out_specs=pl.BlockSpec((experts // 2, deep, LANES), lambda i: (i, 0, 0)),
        out_shape=shape_of((experts, deep, LANES)),
        compiler_params=params(),
        cost_estimate=costs(5),
    )(own, arrived, backs, backs_arrived, hidden, hidden_arrived)


def unpacked(terms, units, tall):
    tiles, tail = 3 * units // LANES, 3 * units % LANES
    whole = terms[: tiles * tall].reshape(tiles, tall, LANES).transpose(1, 0, 2)
    return jnp.concatenate(
        [whole.reshape(tall, tiles * LANES), terms[tiles * tall :, :tall].T], axis=1
    )


def expert_kernel(
    capacity,
    coords_ref,
    slices_ref,
    gate_own_ref,
    gate_other_ref,
    up_own_ref,
    up_other_ref,
    down_own_ref,
    down_other_ref,
    rows_in_ref,
    scaled_out_ref,
    sent_ref,
    hidden_ref,
    backs_ref,
    pre,
    from_down,
    folded,
    scale,
    folds,
):
    step = pl.program_id(0)
    quarters = pl.num_programs(0) // 2
    pair, main, _ = slices_ref.shape
    block = gate_own_ref.shape[1]
    units = hidden_ref.shape[1]
    feats = block // pair
    piece = feats * 2 // quarters
    rest = rows_in_ref.shape[0] - main
    left = capacity - TILE
    owned = lax.rem(step, quarters) < quarters // 2
    place = lax.rem(coords_ref[1] * (quarters // 2) + step, quarters)

    @pl.when(step == 0)
    def _():
        pre[...] = jnp.zeros_like(pre)
        from_down[...] = jnp.zeros_like(from_down)
        folded[...] = jnp.zeros_like(folded)
        source = lax.broadcasted_iota(jnp.int32, (main, rest), 1)
        target = lax.broadcasted_iota(jnp.int32, (main, rest), 0)
        first = source // left * TILE + source % left
        for quarter in range(quarters):
            folds[quarter] = select(target == first + quarter * left)

    def forward(gate_ref, up_ref, down_ref):
        pair_rows = jnp.concatenate([gate_ref[...], up_ref[...]], axis=0)
        parts = [slices_ref[part] for part in range(pair)]

        @pl.when(step == 0)
        def _():
            scales = parts[0][:, 2 * feats + piece :]
            scale[:main] = scales[:, 0:1].astype(F32)
            scale[main:] = contract(folds[0], scales, 0, 0)[:, 1:2]

        rows_in_ref[:main] = jnp.concatenate([part[:, :feats] for part in parts], axis=1)
        rows_out = jnp.concatenate([part[:, feats : 2 * feats] for part in parts], axis=1)
        beside = jnp.concatenate(
            [part[:, 2 * feats : 2 * feats + piece] for part in parts], axis=1
        )
        spread = [contract(folds[quarter], beside, 0, 0).astype(BF16) for quarter in range(quarters)]
        half = quarters // 2

        def unfolded(which):
            return jnp.concatenate(
                [
                    spread[which * half + quarter][:, part * piece : (part + 1) * piece]
                    for part in range(pair)
                    for quarter in range(half)
                ],
                axis=1,
            )

        rows_in_ref[main:] = unfolded(0)
        rows_out = jnp.concatenate([rows_out, unfolded(1)], axis=0)
        scaled_out_ref[...] = (scale[...] * rows_out.astype(F32)).astype(BF16)
        pre[...] += contract(rows_in_ref[...], pair_rows, 1, 1)
        from_down[...] += contract(rows_out, down_ref[...], 1, 1)

    @pl.when((step < quarters) & owned)
    def _():
        forward(gate_own_ref, up_own_ref, down_own_ref)

    @pl.when((step < quarters) & jnp.logical_not(owned))
    def _():
        forward(gate_other_ref, up_other_ref, down_other_ref)

    @pl.when(step == quarters - 1)
    def _():
        back = from_down[...]
        act, slope = sigmoid_parts(pre[:, :units])
        raised = pre[:, units:]
        hidden = (act * raised).astype(BF16)
        hidden_ref[...] = hidden
        scaled = scale[...] * back
        backs_ref[...] = jnp.concatenate(
            [(scaled * raised * slope).astype(BF16), (scaled * act).astype(BF16)], axis=1
        )
        probe = jnp.sum(hidden.astype(F32) * back, axis=1, keepdims=True)
        high = probe.astype(BF16).astype(F32)
        low = probe - high
        lane = lax.broadcasted_iota(jnp.int32, (main, LANES), 1)
        beside = jnp.where(lane == 0, high[:main], jnp.where(lane == 1, low[:main], 0.0))
        lane = lax.broadcasted_iota(jnp.int32, (rest, LANES), 1)
        after = jnp.where(lane == 2, high[main:], jnp.where(lane == 3, low[main:], 0.0))
        after = jnp.dot(folds[0], after.astype(BF16), preferred_element_type=F32)
        sent_ref[:, sent_ref.shape[1] - LANES :] = (beside + after).astype(BF16)

    def backward(gate_ref, up_ref):
        pair_rows = jnp.concatenate([gate_ref[...], up_ref[...]], axis=0)
        rows = jnp.dot(backs_ref[...], pair_rows, preferred_element_type=F32).astype(BF16)
        sent_ref[:, pl.ds(pl.multiple_of(place * block, LANES), block)] = rows[:main]
        folded[...] += jnp.dot(folds[place], rows[main:], preferred_element_type=F32)

    @pl.when((step >= quarters) & owned)
    def _():
        backward(gate_own_ref, up_own_ref)

    @pl.when((step >= quarters) & jnp.logical_not(owned))
    def _():
        backward(gate_other_ref, up_other_ref)

    @pl.when(step == 2 * quarters - 1)
    def _():
        sent_ref[:, quarters * block : (quarters + 1) * block] = folded[...].astype(BF16)


def expert_rows(slices, coords, gates, ups, downs, experts, capacity):
    size, main, wide = slices.shape
    units, half_width = downs[0].shape
    width = 2 * half_width
    quarters = TILE // (capacity - TILE)
    block = width // quarters
    rows = experts * capacity
    whole = lambda shape: pl.BlockSpec(shape, lambda i, c: (0, 0))
    last = quarters // 2 - 1

    def early(i, c):
        return (0, lax.rem(c[1] * (quarters // 2) + jnp.minimum(i, quarters - 1), quarters))

    def own(i, c):
        return (0, jnp.minimum(lax.rem(i, quarters), last))

    def other(i, c):
        return (0, jnp.maximum(lax.rem(i, quarters), last + 1) - last - 1)

    def own_once(i, c):
        return (0, jnp.minimum(i, last))

    def other_once(i, c):
        return (0, jnp.clip(i - last - 1, 0, last))

    return pl.pallas_call(
        functools.partial(expert_kernel, capacity),
        grid_spec=pltpu.PrefetchScalarGridSpec(
            num_scalar_prefetch=1,
            grid=(2 * quarters,),
            in_specs=[pl.BlockSpec((size // quarters, main, wide), lambda i, c: early(i, c)[::-1] + (0,))]
            + [pl.BlockSpec((units, block), own), pl.BlockSpec((units, block), other)] * 2
            + [pl.BlockSpec((units, block), own_once), pl.BlockSpec((units, block), other_once)],
            out_specs=[
                pl.BlockSpec((rows, block), early),
                pl.BlockSpec((rows, block), early),
                whole((main, width + block + LANES)),
                whole((rows, units)),
                whole((rows, 2 * units)),
            ],
            scratch_shapes=[
                pltpu.VMEM((rows, 2 * units), F32),
                pltpu.VMEM((rows, units), F32),
                pltpu.VMEM((main, block), F32),
                pltpu.VMEM((rows, 1), F32),
                pltpu.VMEM((quarters, main, rows - main), BF16),
            ],
        ),
        out_shape=[
            shape_of((rows, width)),
            shape_of((rows, width)),
            shape_of((main, width + block + LANES)),
            shape_of((rows, units)),
            shape_of((rows, 2 * units)),
        ],
        compiler_params=params(),
        cost_estimate=costs(16),
    )(coords, slices, *gates, *ups, *downs)


def combine_kernel(
    left,
    coords_ref,
    main_ref,
    folded_ref,
    probe_ref,
    places_ref,
    dense_own_ref,
    dense_other_ref,
    total_ref,
    extra,
):
    step = pl.program_id(0)
    quarters = pl.num_programs(0)
    quarter = lax.rem(coords_ref[1] * (quarters // 2) + step, quarters)
    slots = main_ref.shape[0]
    parts, tall, tokens = total_ref.shape
    feats = tall - TILE
    lane = lax.broadcasted_iota(jnp.int32, (tokens, slots), 1)
    pick = lambda place: select(lane == place)
    near = [pick(places_ref[:, k : k + 1]) for k in range(TOP)]
    far = [places_ref[:, TOP + k : TOP + k + 1] for k in range(TOP)]

    @pl.when(step == 0)
    def _():
        probes = []
        for k in range(TOP):
            first = contract(probe_ref[...], near[k], 0, 1)
            second = contract(probe_ref[...], pick(far[k]), 0, 1)
            probes.append(first[0:1] + first[1:2] + (second[2:3] + second[3:4]))
        probes = jnp.concatenate(probes, axis=0)
        high = probes.astype(BF16).astype(F32)
        empty = jnp.zeros((TILE - 2 * TOP, tokens), F32)
        extra[...] = jnp.concatenate([high, probes - high, empty], axis=0).astype(BF16)

    shifted = [pick(place + quarter * left) for place in far]
    rows = jnp.dot(near[0] + near[1], main_ref[...], preferred_element_type=F32)
    rows += jnp.dot(shifted[0] + shifted[1], folded_ref[...], preferred_element_type=F32)
    dense = jnp.where(step < quarters // 2, dense_own_ref[...], dense_other_ref[...])
    rows = (dense + rows.T).astype(BF16)
    for part in range(parts):
        total_ref[part, :feats, :] = rows[part * feats : (part + 1) * feats]
        total_ref[part, feats:, :] = extra[...]


def combine(back, coords, places, dense_own, dense_other, size, capacity):
    half_width, tokens = dense_own.shape
    width = 2 * half_width
    left = capacity - TILE
    quarters = TILE // left
    block = width // quarters
    slots = back.shape[0]
    feats = width // size
    last = quarters // 2 - 1
    return pl.pallas_call(
        functools.partial(combine_kernel, left),
        grid_spec=pltpu.PrefetchScalarGridSpec(
            num_scalar_prefetch=1,
            grid=(quarters,),
            in_specs=[
                pl.BlockSpec(
                    (slots, block), lambda i, c: (0, lax.rem(c[1] * (quarters // 2) + i, quarters))
                ),
                pl.BlockSpec((slots, block), lambda i, c: (0, quarters)),
                pl.BlockSpec((slots, LANES), lambda i, c: (0, (quarters + 1) * block // LANES)),
                pl.BlockSpec((tokens, 2 * TOP), lambda i, c: (0, 0)),
                pl.BlockSpec((block, tokens), lambda i, c: (jnp.minimum(i, last), 0)),
                pl.BlockSpec((block, tokens), lambda i, c: (jnp.maximum(i, last + 1) - last - 1, 0)),
            ],
            out_specs=pl.BlockSpec(
                (size // quarters, feats + TILE, tokens),
                lambda i, c: (lax.rem(c[1] * (quarters // 2) + i, quarters), 0, 0),
            ),
            scratch_shapes=[pltpu.VMEM((TILE, tokens), BF16)],
        ),
        out_shape=jax.ShapeDtypeStruct((size, feats + TILE, tokens), BF16),
        compiler_params=pltpu.CompilerParams(
            dimension_semantics=("arbitrary",), vmem_limit_bytes=VMEM_LIMIT
        ),
        cost_estimate=costs(6),
    )(coords, back, back, back, places, dense_own, dense_other)


def local(
    layer_input,
    cotangent,
    route_probs,
    routes,
    shared_gate,
    shared_up,
    shared_down,
    routed_gate,
    routed_up,
    routed_down,
):
    tok_rows, feats = layer_input.shape
    experts = lax.axis_size("expert")
    capacity = 5 * TOP * tok_rows // (4 * experts)

    both = jnp.concatenate([layer_input.T, cotangent.T], axis=0)
    coords = jnp.stack([lax.axis_index("tensor"), lax.axis_index("dp")]).astype(jnp.int32)

    def with_other(own):
        return own, swap(own)

    dense_weights = [
        with_other(weight) for weight in (shared_gate.T, shared_up.T, shared_down)
    ]
    expert_weights = [
        with_other(weight) for weight in (routed_gate[0].T, routed_up[0].T, routed_down[0])
    ]

    folded, places = dispatch(routes.T, route_probs.T, both, experts, capacity)
    size = lax.axis_size("tensor")
    arrived = lax.all_to_all(
        folded.reshape(experts, TILE, -1), "expert", split_axis=0, concat_axis=0, tiled=True
    )
    pieces, state = single_ring(both, range(1, size // 2))
    arrived, state, dense_weights = lax.optimization_barrier((arrived, state, dense_weights))
    pieces += single_ring(both, [size // 2], state)[0] + [(both, 0)]
    slices = lax.all_gather(
        arrived.reshape(experts * TILE, -1), "tensor", axis=0, tiled=False
    )

    own_rows, other_rows, dense_backs, dense_hidden = dense_forward(
        pieces, coords, *dense_weights
    )
    terms = dense_terms(
        own_rows,
        swap(other_rows),
        dense_backs,
        swap(dense_backs),
        dense_hidden,
        swap(dense_hidden),
        experts,
    )
    terms = lax.all_to_all(terms, "expert", split_axis=0, concat_axis=0, tiled=True)
    units = dense_hidden.shape[0]
    dense_own, dense_other = [
        product("hd,hn->dn", gate, dense_backs[:units])
        + product("hd,hn->dn", up, dense_backs[units:])
        for gate, up in zip(*dense_weights[:2])
    ]

    slot_in, scaled_out, sent, hidden, backs = expert_rows(
        slices, coords, *expert_weights, experts, capacity
    )
    sent, terms = lax.optimization_barrier((sent, terms))
    terms = terms.astype(F32).sum(axis=0).astype(BF16)
    terms = unpacked(terms, units, own_rows.shape[0] * feats // experts)
    grad_gate = terms[:, :units]
    grad_up = terms[:, units : 2 * units]
    grad_down = terms[:, 2 * units :].T
    back = lax.all_to_all(
        sent.reshape(experts, TILE, -1), "expert", split_axis=0, concat_axis=0, tiled=True
    )

    def reduced(rows, backs):
        own, other = halves(rows, 1)
        arrived = swap(product("sh,sd->hd", backs, other).astype(BF16))
        return (product("sh,sd->hd", backs, own) + arrived.astype(F32)).astype(BF16)

    delta_pair = reduced(slot_in, backs)
    delta_gate = delta_pair[:units].T[None]
    delta_up = delta_pair[units:].T[None]
    delta_down = reduced(scaled_out, hidden)[None]

    total = combine(
        back.reshape(experts * TILE, -1),
        coords,
        places,
        dense_own,
        dense_other,
        lax.axis_size("tensor"),
        capacity,
    )
    total = lax.all_to_all(total, "tensor", split_axis=0, concat_axis=0, tiled=True)
    total = total.astype(F32).sum(axis=0)
    input_grad = total[:feats].T.astype(BF16)
    prob_grad = (total[feats : feats + TOP] + total[feats + TOP : feats + 2 * TOP]).T
    return (
        input_grad,
        prob_grad,
        grad_gate,
        grad_up,
        grad_down,
        delta_gate,
        delta_up,
        delta_down,
    )


def solution(mesh):
    return jax.shard_map(
        local,
        mesh=mesh,
        in_specs=(
            P(("dp", "expert"), "tensor"),
            P(("dp", "expert"), "tensor"),
            P(("dp", "expert"), None),
            P(("dp", "expert"), None),
            P("dp", "tensor"),
            P("dp", "tensor"),
            P("tensor", "dp"),
            P("expert", "dp", "tensor"),
            P("expert", "dp", "tensor"),
            P("expert", "tensor", "dp"),
        ),
        out_specs=(
            P(("dp", "expert"), "tensor"),
            P(("dp", "expert"), None),
            P(("dp", "expert"), "tensor"),
            P(("dp", "expert"), "tensor"),
            P("tensor", ("dp", "expert")),
            P("expert", "dp", "tensor"),
            P("expert", "dp", "tensor"),
            P("expert", "tensor", "dp"),
        ),
        check_vma=False,
    )
```
